512 devices in a mesh: row: 32 (over z, core), col: 16 (over x, y).
Axes of the slice: x: 4, y: 4, z: 16, core: 2. Of those that a mesh axis runs over, the one named last changes fastest.
Arguments:
- currents: float32 [96, 8192], P(None, ('row', 'col')), may hold values from -6 to 6
- residual: float32 [96, 8192], P(None, ('row', 'col')), may hold values from -6 to 6
- shadow: float32 [96, 8192], P(None, ('row', 'col')), may hold values from -6 to 6
- lattice_sites: int32 [3, 8192], P(None, ('row', 'col')), may hold values from 0 to 127, as said below
- classes: int32 [8192], P(('row', 'col')), may hold values from 0 to 3
- inverse_polarizability: float32 [2, 4], replicated, may hold values from 2 to 6
Outputs:
- image: float32 [96, 8192], P(None, ('row', 'col'))
- half_step: float32 [96, 8192], P(None, ('row', 'col'))
The draws below stay inside these ranges and needn't reach their ends.
Inputs may be any that keep to these rules, and one draw needn't show every extreme that they name: `lattice_sites`: every site of the lattice with x below 32, y below 128 and z 0 or 1 holds exactly one dipole; no two dipoles share a site.
All inputs are finite; a program needn't handle non-finite values.
Results may differ from the reference program's by a relative error of at most 0.0003.
Values sent between devices are 32-bit elements; how exact they have to be, the bound alone decides.
A program may use at most 64 MiB of HBM per device.

```python
import jax
import jax.numpy as jnp
from jax import lax

RHS = 16
NCLASS = 4
LATX = 32
N = 8192


def draw_lattice_sites(key, part):
    key = jax.random.fold_in(key, 7)
    ordering = jax.random.permutation(key, N)
    layer_size = N // 2
    first_axis = ordering % LATX
    second_axis = ordering % layer_size // LATX
    layer_index = ordering // layer_size
    return jnp.stack([first_axis, second_axis, layer_index]).astype(jnp.int32)


def set_ends(values, stream_key, low, top_value):
    index_at = [jax.random.randint(jax.random.fold_in(stream_key, axis), (), 0, length) for axis, length in enumerate(values.shape)]
    widest = values.shape.index(max(values.shape))
    beside = index_at[:widest] + [(index_at[widest] + 1) % values.shape[widest]] + index_at[widest + 1:]
    return values.at[tuple(index_at)].set(low).at[tuple(beside)].set(top_value)


def steps_of(stream_key, extent, pieces, least, largest):
    factor_of, own = 1.0, jax.random.fold_in(stream_key, 6)
    for position, parts in pieces:
        steps = jnp.exp(jax.random.uniform(jax.random.fold_in(own, position), (parts,), jnp.float32, least / len(pieces), largest / len(pieces)))
        factor_of = factor_of * jnp.repeat(steps, extent[position] // parts).reshape([-1 if axis == position else 1 for axis in range(len(extent))])
    return factor_of


def noise(rng, shape, scale, most, pieces=(), kind=jnp.bfloat16):
    entries = jax.random.normal(rng, shape, jnp.float32) * scale
    if len(pieces) > 0:
        entries = steps_of(rng, shape, pieces, -0.22, 0.18) * entries
    return jnp.clip(entries, min=-most, max=most).astype(kind)


def setup_inputs(seed: int = 0) -> dict:
    key_of = jax.random.split(jax.random.key(seed), 7)
    return {
        "currents": noise(key_of[0], (6 * RHS, N), 1.0, 6.0, ((1, 512),), jnp.float32),
        "residual": noise(key_of[1], (6 * RHS, N), 1.0, 6.0, ((1, 512),), jnp.float32),
        "shadow": noise(key_of[2], (6 * RHS, N), 1.0, 6.0, ((1, 512),), jnp.float32),
        "lattice_sites": draw_lattice_sites(jax.random.fold_in(key_of[6], 71), 0),
        "classes": set_ends(jax.random.randint(key_of[4], (N,), 0, NCLASS), jax.random.fold_in(key_of[4], 1), 0, NCLASS - 1).astype(jnp.int32),
        "inverse_polarizability": jnp.clip(jax.random.uniform(key_of[5], (2, NCLASS), jnp.float32, 2.0, 6.0), 2.0, 6.0),
    }


wavenumber = 0.9

def green_apply(target_sites, source_sites, source_flows):
    separation = target_sites[:, :, None] - source_sites[:, None, :]
    distance_sq = lax.optimization_barrier(jnp.sum(separation * separation, axis=0))
    present = distance_sq > 0.5
    distance = jnp.sqrt(jnp.where(present, distance_sq, 1.0))
    inverse = 1.0 / distance
    unit_dir = separation * inverse
    phase_cos = jnp.cos(wavenumber * distance)
    phase_sin = jnp.sin(wavenumber * distance)
    reach = jnp.where(present, inverse, 0.0)
    iso_real = wavenumber * wavenumber - inverse * inverse
    iso_imag = wavenumber * inverse
    dyad_real = 3.0 * inverse * inverse - wavenumber * wavenumber
    dyad_imag = -3.0 * wavenumber * inverse
    iso_re = (phase_cos * iso_real - phase_sin * iso_imag) * reach
    iso_im = (phase_sin * iso_real + phase_cos * iso_imag) * reach
    dyad_re = (phase_cos * dyad_real - phase_sin * dyad_imag) * reach
    dyad_im = (phase_sin * dyad_real + phase_cos * dyad_imag) * reach
    identity = jnp.eye(3, dtype=jnp.float32)[:, :, None, None]
    outer = unit_dir[:, None] * unit_dir[None, :]
    tensor_re = identity * iso_re + outer * dyad_re
    tensor_im = identity * iso_im + outer * dyad_im
    flows = source_flows.reshape(2, 3, -1, source_flows.shape[1])
    real_part = jnp.einsum('cdts,bdks->bckt', tensor_re, flows, precision=lax.Precision.HIGHEST)
    imag_part = jnp.einsum('cdts,bdks->bckt', tensor_im, flows, precision=lax.Precision.HIGHEST)
    field = jnp.stack([real_part[0] - imag_part[1], real_part[1] + imag_part[0]])
    return field.reshape(source_flows.shape[0], target_sites.shape[1])

def finish(currents, residual, shadow, fields, classes, inverse_polarizability):
    planes = currents.shape[0]
    owned = currents.shape[1]
    flows4 = currents.reshape(2, 3, -1, owned)
    fields4 = fields.reshape(2, 3, -1, owned)
    onehot = (classes[None, :] == jnp.arange(inverse_polarizability.shape[1], dtype=jnp.int32)[:, None]).astype(jnp.float32)
    pol_re = lax.optimization_barrier(jnp.sum(inverse_polarizability[0][:, None] * onehot, axis=0))
    pol_im = lax.optimization_barrier(jnp.sum(inverse_polarizability[1][:, None] * onehot, axis=0))
    image_re = pol_re * flows4[0] - pol_im * flows4[1] - fields4[0]
    image_im = pol_re * flows4[1] + pol_im * flows4[0] - fields4[1]
    return (image_re, image_im)

def paired(shadow4, other_re, other_im):
    real_sum = lax.optimization_barrier(jnp.sum(shadow4[0] * other_re + shadow4[1] * other_im, axis=(0, 2)))
    imag_sum = lax.optimization_barrier(jnp.sum(shadow4[0] * other_im - shadow4[1] * other_re, axis=(0, 2)))
    return (real_sum, imag_sum)

def update(residual, image_re, image_im, rho_re, rho_im, den_re, den_im):
    owned = residual.shape[1]
    resid4 = residual.reshape(2, 3, -1, owned)
    magnitude = jnp.maximum(den_re * den_re + den_im * den_im, 1.0)
    alpha_re = ((rho_re * den_re + rho_im * den_im) / magnitude)[None, :, None]
    alpha_im = ((rho_im * den_re - rho_re * den_im) / magnitude)[None, :, None]
    half_re = resid4[0] - (alpha_re * image_re - alpha_im * image_im)
    half_im = resid4[1] - (alpha_re * image_im + alpha_im * image_re)
    image_out = jnp.stack([image_re, image_im]).reshape(residual.shape)
    return (image_out, jnp.stack([half_re, half_im]).reshape(residual.shape))

def reference(currents, residual, shadow, lattice_sites, classes, inverse_polarizability):
    places = lattice_sites.astype(jnp.float32)
    planes = currents.shape[0]
    target_len = min(512, N)
    source_len = min(1024, N)

    def one_target(target_idx):
        targets = lax.dynamic_slice_in_dim(places, target_idx * target_len, target_len, 1)

        def adding(running, source_idx):
            spots = lax.dynamic_slice_in_dim(places, source_idx * source_len, source_len, 1)
            flows = lax.dynamic_slice_in_dim(currents, source_idx * source_len, source_len, 1)
            return (running + green_apply(targets, spots, flows), None)
        summed, unused = lax.scan(adding, jnp.zeros((planes, target_len), jnp.float32), jnp.arange(N // source_len, dtype=jnp.int32))
        return summed
    mapped = lax.map(one_target, jnp.arange(N // target_len, dtype=jnp.int32))
    fields = jnp.transpose(mapped, (1, 0, 2)).reshape(planes, N)
    image_re, image_im = finish(currents, residual, shadow, fields, classes, inverse_polarizability)
    shadow4 = shadow.reshape(2, 3, -1, N)
    resid4 = residual.reshape(2, 3, -1, N)
    rho_re, rho_im = paired(shadow4, resid4[0], resid4[1])
    den_re, den_im = paired(shadow4, image_re, image_im)
    return update(residual, image_re, image_im, rho_re, rho_im, den_re, den_im)
```

```python
import functools
import math

import jax
import jax.numpy as jnp
import numpy as np
from jax import lax
from jax.experimental import pallas as pl
from jax.experimental.pallas import tpu as pltpu
from jax.sharding import PartitionSpec as P

MESH = pl.DeviceIdType.MESH
K = 0.9
SH = 16
PLANES = 96
PAIRS = ((0, 0), (1, 1), (2, 2), (0, 1), (0, 2), (1, 2))


def _fit(terms, odd):
    nodes = 0.5 * np.cos((np.arange(400) + 0.5) * np.pi / 400)
    powers = np.arange(terms) * 2 + (1 if odd else 0)
    values = np.sin(2 * np.pi * nodes) if odd else np.cos(2 * np.pi * nodes)
    solved = np.linalg.lstsq(nodes[:, None] ** powers[None, :], values, rcond=None)[0]
    return [float(x) for x in solved]


SIN = _fit(6, True)
COS = _fit(7, False)


def _horner(coefs, x):
    out = jnp.float32(coefs[-1])
    for coef in coefs[-2::-1]:
        out = out * x + jnp.float32(coef)
    return out


def green(tx, ty, tz, sx, sy, sz):
    dx, dy, dz = tx - sx, ty - sy, tz - sz
    xx, yy, zz = dx * dx, dy * dy, dz * dz
    dist_sq = xx + yy + zz
    safe = jnp.maximum(dist_sq, 1.0)
    inv = lax.rsqrt(safe)
    dist = safe * inv
    reach = inv * jnp.minimum(dist_sq, 1.0)
    turns = dist * jnp.float32(K / (2 * math.pi))
    frac = turns - jnp.round(turns)
    frac_sq = frac * frac
    e_re = _horner(COS, frac_sq) * reach
    e_im = _horner(SIN, frac_sq) * frac * reach
    inv_sq = inv * inv
    iso_re = jnp.float32(K * K) - inv_sq
    iso_im = jnp.float32(K) * inv
    a_re = e_re * iso_re - e_im * iso_im
    a_im = e_im * iso_re + e_re * iso_im
    b_re = (jnp.float32(2 * K * K) * e_re - 3.0 * a_re) * inv_sq
    b_im = (jnp.float32(2 * K * K) * e_im - 3.0 * a_im) * inv_sq
    outer = (xx, yy, zz, dx * dy, dx * dz, dy * dz)
    parts = []
    for place, product in enumerate(outer):
        re, im = product * b_re, product * b_im
        if place < 3:
            re, im = re + a_re, im + a_im
        parts.extend((re, im))
    return parts


def rows(array, b, component):
    start = b * 48 + component * 16
    return array[start : start + 16]


def dots(left_re, left_im, right_re, right_im):
    return left_re * right_re + left_im * right_im, left_re * right_im - left_im * right_re


def body(
    R, C,
    cur_hbm, res_hbm, sha_hbm, site_hbm, cls_hbm, pol_hbm,
    img_out, half_out,
    cur, res, sha, site, cls, pol,
    stage, src_all, tgt_all, tgt_t, ghi, glo, rs_send, rs_recv, fin_all,
    in_sems, send_sems, recv_sems,
):
    r, c = lax.axis_index("row"), lax.axis_index("col")
    T, S = C * SH, R * SH
    pairs = ((cur_hbm, cur), (res_hbm, res), (sha_hbm, sha), (site_hbm, site), (cls_hbm, cls), (pol_hbm, pol))
    loads = [pltpu.make_async_copy(a, b, in_sems.at[i]) for i, (a, b) in enumerate(pairs)]
    for load in loads:
        load.start()

    barrier = pltpu.get_barrier_semaphore()

    def greet_row(i, carry):
        pl.semaphore_signal(barrier, inc=1, device_id={"row": lax.rem(r + i, R)}, device_id_type=MESH)
        return carry

    def greet_col(i, carry):
        pl.semaphore_signal(barrier, inc=1, device_id={"col": lax.rem(c + i, C)}, device_id_type=MESH)
        return carry

    lax.fori_loop(1, R, greet_row, 0)
    lax.fori_loop(1, C, greet_col, 0)

    stage[...] = jnp.zeros_like(stage)
    for load in loads:
        load.wait()

    stage[0:PLANES, 0:SH] = cur[...]
    stage[PLANES : PLANES + 3, 0:SH] = site[...].astype(jnp.float32)
    src_all[r] = stage[...].T[0:SH]
    stage[0:PLANES, 0:SH] = sha[...]
    tgt_all[c] = stage[...].T[0:SH]
    pl.semaphore_wait(barrier, R + C - 2)

    def send_src(i, carry):
        pltpu.make_async_remote_copy(
            src_ref=src_all.at[r], dst_ref=src_all.at[r], send_sem=send_sems.at[0], recv_sem=recv_sems.at[0],
            device_id={"row": lax.rem(r + i, R)}, device_id_type=MESH,
        ).start()
        return carry

    def send_tgt(i, carry):
        pltpu.make_async_remote_copy(
            src_ref=tgt_all.at[c], dst_ref=tgt_all.at[c], send_sem=send_sems.at[1], recv_sem=recv_sems.at[1],
            device_id={"col": lax.rem(c + i, C)}, device_id_type=MESH,
        ).start()
        return carry

    def drained(buffer, count, which):
        whole = buffer.at[pl.ds(0, count)]
        return pltpu.make_async_remote_copy(
            src_ref=whole, dst_ref=whole, send_sem=send_sems.at[which], recv_sem=recv_sems.at[which],
            device_id={"row": lax.rem(r + 1, R)}, device_id_type=MESH,
        )

    lax.fori_loop(1, C, send_tgt, 0)
    lax.fori_loop(1, R, send_src, 0)

    class_id = cls[...]
    pol_re = jnp.zeros((1, SH), jnp.float32)
    pol_im = jnp.zeros((1, SH), jnp.float32)
    for kind in range(pol.shape[1]):
        pol_re = jnp.where(class_id == kind, pol[0:1, kind : kind + 1], pol_re)
        pol_im = jnp.where(class_id == kind, pol[1:2, kind : kind + 1], pol_im)
    own_re, own_im = [], []
    den_re = den_im = rho_re = rho_im = 0.0
    for comp in range(3):
        cr, ci = rows(cur, 0, comp), rows(cur, 1, comp)
        sr, si = rows(sha, 0, comp), rows(sha, 1, comp)
        own_re.append(pol_re * cr - pol_im * ci)
        own_im.append(pol_re * ci + pol_im * cr)
        re, im = dots(sr, si, own_re[-1], own_im[-1])
        den_re, den_im = den_re + re, den_im + im
        re, im = dots(sr, si, rows(res, 0, comp), rows(res, 1, comp))
        rho_re, rho_im = rho_re + re, rho_im + im
    own_den_re, own_den_im, rho_re, rho_im = (
        jnp.sum(x, axis=1, keepdims=True) for x in (den_re, den_im, rho_re, rho_im)
    )

    drained(tgt_all, C - 1, 1).wait()
    tgt_t[...] = tgt_all[...].reshape(T, 128).T
    tx, ty, tz = (tgt_t[PLANES + i : PLANES + i + 1, :] for i in range(3))
    drained(src_all, R - 1, 0).wait()

    def fill(j, carry):
        block = src_all[j]
        sx, sy, sz = (block[:, PLANES + i : PLANES + i + 1] for i in range(3))
        place = pl.ds(pl.multiple_of(j * SH, SH), SH)
        for which, value in enumerate(green(tx, ty, tz, sx, sy, sz)):
            high = value.astype(jnp.bfloat16)
            ghi[which, place, :] = high
            glo[which, place, :] = (value - high.astype(jnp.float32)).astype(jnp.bfloat16)
        return carry

    lax.fori_loop(0, R, fill, 0)

    flows = src_all[...].reshape(S, 128).T
    f_hi = flows.astype(jnp.bfloat16)
    f_lo = (flows - f_hi.astype(jnp.float32)).astype(jnp.bfloat16)

    def two(array, comp):
        return [rows(array, 0, comp), rows(array, 1, comp)]

    sums = [[0.0, 0.0, 0.0], [0.0, 0.0, 0.0]]
    for which, (a, b) in enumerate(PAIRS):
        high = two(f_hi, a) if a == b else two(f_hi, b) + two(f_hi, a)
        low = two(f_lo, a) if a == b else two(f_lo, b) + two(f_lo, a)
        height = 16 * len(high)
        both = jnp.concatenate(high + low, axis=0)
        high = both[:height]
        for part in range(2):
            one = jnp.dot(both, ghi[2 * which + part], preferred_element_type=jnp.float32)
            other = jnp.dot(high, glo[2 * which + part], preferred_element_type=jnp.float32)
            got = one[:height] + one[height:] + other
            sums[part][a] = sums[part][a] + got[:32]
            if a != b:
                sums[part][b] = sums[part][b] + got[32:]

    field_re = [sums[0][i][:16] - sums[1][i][16:] for i in range(3)]
    field_im = [sums[0][i][16:] + sums[1][i][:16] for i in range(3)]
    den_re = den_im = 0.0
    for comp in range(3):
        re, im = dots(rows(tgt_t, 0, comp), rows(tgt_t, 1, comp), field_re[comp], field_im[comp])
        den_re, den_im = den_re + re, den_im + im
    den_re = own_den_re - jnp.sum(den_re, axis=1, keepdims=True)
    den_im = own_den_im - jnp.sum(den_im, axis=1, keepdims=True)
    early = lax.broadcasted_iota(jnp.int32, (16, T), 1) % 16 < 8
    tail_re = jnp.where(early, den_re, rho_re)
    tail_im = jnp.where(early, den_im, rho_im)
    partial = jnp.concatenate(field_re + field_im + [tail_re, tail_im], axis=0)
    rs_send[...] = partial.T.reshape(C, SH, 128)

    def send_field(i, carry):
        peer = lax.rem(c + i, C)
        pltpu.make_async_remote_copy(
            src_ref=rs_send.at[peer], dst_ref=rs_recv.at[c], send_sem=send_sems.at[2], recv_sem=recv_sems.at[2],
            device_id={"col": peer}, device_id_type=MESH,
        ).start()
        return carry

    lax.fori_loop(1, C, send_field, 0)
    rs_recv[c] = rs_send[c]
    drained(rs_recv, C - 1, 2).wait()
    total = jnp.sum(rs_recv[...], axis=0)
    lane = lax.broadcasted_iota(jnp.int32, (8, 128), 1)
    fin_all[r] = jnp.where(lane >= 96, total[0:8], pltpu.roll(total[8:16], 96, 1))[0:1]

    def send_fin(i, carry):
        pltpu.make_async_remote_copy(
            src_ref=fin_all.at[r], dst_ref=fin_all.at[r], send_sem=send_sems.at[3], recv_sem=recv_sems.at[3],
            device_id={"row": lax.rem(r + i, R)}, device_id_type=MESH,
        ).start()
        return carry

    lax.fori_loop(1, R, send_fin, 0)

    stage[0:SH, :] = total
    field = stage[...].T[:, 0:SH]
    image_re = [own_re[i] - rows(field, 0, i) for i in range(3)]
    image_im = [own_im[i] - rows(field, 1, i) for i in range(3)]
    img_out[...] = jnp.concatenate(image_re + image_im, axis=0)

    drained(fin_all, R - 1, 3).wait()
    ends = jnp.sum(fin_all[...], axis=0)
    lane = lax.broadcasted_iota(jnp.int32, (16, 128), 1)
    angle = lax.broadcasted_iota(jnp.int32, (16, 128), 0)

    def column(start):
        return jnp.sum(jnp.where(lane == angle + start, ends, 0.0), axis=1, keepdims=True)

    rho_re, rho_im, den_re, den_im = column(64), column(80), column(96), column(112)
    magnitude = jnp.maximum(den_re * den_re + den_im * den_im, 1.0)
    alpha_re = (rho_re * den_re + rho_im * den_im) / magnitude
    alpha_im = (rho_im * den_re - rho_re * den_im) / magnitude
    half_re = [rows(res, 0, i) - (alpha_re * image_re[i] - alpha_im * image_im[i]) for i in range(3)]
    half_im = [rows(res, 1, i) - (alpha_re * image_im[i] + alpha_im * image_re[i]) for i in range(3)]
    half_out[...] = jnp.concatenate(half_re + half_im, axis=0)


def local(R, C, currents, residual, shadow, lattice_sites, classes, inverse_polarizability):
    f32 = jnp.float32
    T, S = C * SH, R * SH
    shape = jax.ShapeDtypeStruct((PLANES, SH), f32)
    return pl.pallas_call(
        functools.partial(body, R, C),
        out_shape=(shape, shape),
        in_specs=[pl.BlockSpec(memory_space=pl.ANY)] * 6,
        out_specs=(pl.BlockSpec(memory_space=pltpu.VMEM), pl.BlockSpec(memory_space=pltpu.VMEM)),
        scratch_shapes=[
            pltpu.VMEM((PLANES, SH), f32),
            pltpu.VMEM((PLANES, SH), f32),
            pltpu.VMEM((PLANES, SH), f32),
            pltpu.VMEM((3, SH), jnp.int32),
            pltpu.VMEM((1, SH), jnp.int32),
            pltpu.VMEM(inverse_polarizability.shape, f32),
            pltpu.VMEM((128, 128), f32),
            pltpu.VMEM((R, SH, 128), f32),
            pltpu.VMEM((C, SH, 128), f32),
            pltpu.VMEM((128, T), f32),
            pltpu.VMEM((12, S, T), jnp.bfloat16),
            pltpu.VMEM((12, S, T), jnp.bfloat16),
            pltpu.VMEM((C, SH, 128), f32),
            pltpu.VMEM((C, SH, 128), f32),
            pltpu.VMEM((R, 1, 128), f32),
            pltpu.SemaphoreType.DMA((6,)),
            pltpu.SemaphoreType.DMA((4,)),
            pltpu.SemaphoreType.DMA((4,)),
        ],
        compiler_params=pltpu.CompilerParams(
            collective_id=0, has_side_effects=True, vmem_limit_bytes=32 * 1024 * 1024
        ),
    )(currents, residual, shadow, lattice_sites, classes.reshape(1, SH), inverse_polarizability)


def solution(mesh):
    both = ("row", "col")
    in_specs = (P(None, both), P(None, both), P(None, both), P(None, both), P(both), P())
    out_specs = (P(None, both), P(None, both))
    step = functools.partial(local, mesh.shape["row"], mesh.shape["col"])
    return jax.shard_map(step, mesh=mesh, in_specs=in_specs, out_specs=out_specs, check_vma=False)
```

```python
import functools
import math

import jax
import jax.numpy as jnp
import numpy as np
from jax import lax
from jax.experimental import pallas as pl
from jax.experimental.pallas import tpu as pltpu
from jax.sharding import PartitionSpec as P

MESH = pl.DeviceIdType.MESH
K = 0.9
SH = 16
PLANES = 96
PAIRS = ((0, 0), (1, 1), (2, 2), (0, 1), (0, 2), (1, 2))


def _fit(terms, odd):
    nodes = 0.5 * np.cos((np.arange(400) + 0.5) * np.pi / 400)
    powers = np.arange(terms) * 2 + (1 if odd else 0)
    values = np.sin(2 * np.pi * nodes) if odd else np.cos(2 * np.pi * nodes)
    solved = np.linalg.lstsq(nodes[:, None] ** powers[None, :], values, rcond=None)[0]
    return [float(x) for x in solved]


SIN = _fit(6, True)
COS = _fit(7, False)


def _horner(coefs, x):
    out = jnp.float32(coefs[-1])
    for coef in coefs[-2::-1]:
        out = out * x + jnp.float32(coef)
    return out


def green(tx, ty, tz, sx, sy, sz):
    dx, dy, dz = tx - sx, ty - sy, tz - sz
    xx, yy, zz = dx * dx, dy * dy, dz * dz
    dist_sq = xx + yy + zz
    safe = jnp.maximum(dist_sq, 1.0)
    inv = lax.rsqrt(safe)
    dist = safe * inv
    reach = inv * jnp.minimum(dist_sq, 1.0)
    turns = dist * jnp.float32(K / (2 * math.pi))
    frac = turns - jnp.round(turns)
    frac_sq = frac * frac
    e_re = _horner(COS, frac_sq) * reach
    e_im = _horner(SIN, frac_sq) * frac * reach
    inv_sq = inv * inv
    iso_re = jnp.float32(K * K) - inv_sq
    iso_im = jnp.float32(K) * inv
    a_re = e_re * iso_re - e_im * iso_im
    a_im = e_im * iso_re + e_re * iso_im
    b_re = (jnp.float32(2 * K * K) * e_re - 3.0 * a_re) * inv_sq
    b_im = (jnp.float32(2 * K * K) * e_im - 3.0 * a_im) * inv_sq
    outer = (xx, yy, zz, dx * dy, dx * dz, dy * dz)
    parts = []
    for place, product in enumerate(outer):
        re, im = product * b_re, product * b_im
        if place < 3:
            re, im = re + a_re, im + a_im
        parts.extend((re, im))
    return parts


def rows(array, b, component):
    start = b * 48 + component * 16
    return array[start : start + 16]


def lanes(height):
    return lax.broadcasted_iota(jnp.int32, (height, 128), 1)


def sublanes(height):
    return lax.broadcasted_iota(jnp.int32, (height, 128), 0)


def swapped(block):
    lane = lanes(block.shape[0])
    turned = jnp.where(lane < 48, -pltpu.roll(block, 80, 1), pltpu.roll(block, 48, 1))
    return jnp.where(lane < PLANES, turned, 0.0)


def fold(block):
    for shift in (64, 32, 16):
        block = block + pltpu.roll(block, shift, 1)
    return block


def body(
    Z, C,
    cur_hbm, res_hbm, sha_hbm, site_hbm, cls_hbm, pol_hbm,
    img_out, half_out,
    cur, res, sha, site, cls, pol,
    wide, src_all, spot_all, tgt_all, tgt_t, ghi, glo, rs_send, rs_recv, den_all, fin_all,
    in_sems, send_sems, recv_sems,
):
    r, c = lax.axis_index("row"), lax.axis_index("col")
    z, core = r // 2, r % 2
    D = 2 * C
    q = core * C + c
    T, S = D * SH, Z * SH

    def plane_peer(i):
        other = lax.rem(q + i, D)
        return other, {"row": z * 2 + other // C, "col": other % C}

    def far_peer(i):
        step = jnp.where(i % 2 == 1, Z // 2 + i // 2, Z // 2 - i // 2)
        return {"row": lax.rem(z + step, Z) * 2 + core}

    pairs = ((cur_hbm, cur), (res_hbm, res), (sha_hbm, sha), (site_hbm, site), (cls_hbm, cls), (pol_hbm, pol))
    loads = [pltpu.make_async_copy(a, b, in_sems.at[i]) for i, (a, b) in enumerate(pairs)]
    for load in loads:
        load.start()

    barrier = pltpu.get_barrier_semaphore()

    def greet_far(i, carry):
        pl.semaphore_signal(barrier, inc=1, device_id=far_peer(i), device_id_type=MESH)
        return carry

    def greet_plane(i, carry):
        pl.semaphore_signal(barrier, inc=1, device_id=plane_peer(i)[1], device_id_type=MESH)
        return carry

    lax.fori_loop(1, Z, greet_far, 0)
    lax.fori_loop(1, D, greet_plane, 0)

    wide[...] = jnp.zeros_like(wide)
    for load in loads:
        load.wait()

    for i, ref in enumerate((cur, res, sha)):
        wide[i, :, 0:PLANES] = ref[...]
    lane, sublane = lanes(SH), sublanes(SH)
    group, diagonal = lane // 16, lane % 16 == sublane
    small_lane = lax.broadcasted_iota(jnp.int32, (SH, SH), 1)
    small_sublane = lax.broadcasted_iota(jnp.int32, (SH, SH), 0)

    def column(row):
        return jnp.sum(jnp.where(small_lane == small_sublane, row, 0.0), axis=1, keepdims=True)

    flow, resid, shade = wide[0], wide[1], wide[2]
    spots = site[...].astype(jnp.float32)
    axes = [column(spots[i : i + 1]) for i in range(3)]
    block = shade
    spot_row = jnp.zeros((SH, 128), jnp.float32)
    for i in range(3):
        block = jnp.where(lane == PLANES + i, axes[i], block)
        spot_row = jnp.where((group == i) & diagonal, axes[i], spot_row)
    tgt_all[q] = block
    spot_all[z] = jnp.sum(spot_row, axis=0, keepdims=True)
    src_all[z] = flow

    def copy(which, src, dst, device_id):
        return pltpu.make_async_remote_copy(
            src_ref=src, dst_ref=dst, send_sem=send_sems.at[which], recv_sem=recv_sems.at[which],
            device_id=device_id, device_id_type=MESH,
        )

    def send_spot(i, carry):
        copy(0, spot_all.at[z], spot_all.at[z], far_peer(i)).start()
        return carry

    def send_tgt(i, carry):
        copy(1, tgt_all.at[q], tgt_all.at[q], plane_peer(i)[1]).start()
        return carry

    def send_src(i, carry):
        copy(2, src_all.at[z], src_all.at[z], far_peer(i)).start()
        return carry

    def drain(which, buffer, count):
        whole = buffer.at[pl.ds(0, count)]
        copy(which, whole, whole, far_peer(1)).wait()

    pl.semaphore_wait(barrier, Z + D - 2)
    lax.fori_loop(1, Z, send_spot, 0)
    lax.fori_loop(1, D, send_tgt, 0)
    lax.fori_loop(1, Z, send_src, 0)

    class_col = column(cls[...].astype(jnp.float32))
    pol_re = jnp.zeros((SH, 1), jnp.float32)
    pol_im = jnp.zeros((SH, 1), jnp.float32)
    for kind in range(pol.shape[1]):
        pol_re = jnp.where(class_col == kind, pol[0:1, kind : kind + 1], pol_re)
        pol_im = jnp.where(class_col == kind, pol[1:2, kind : kind + 1], pol_im)
    own = pol_re * flow + pol_im * swapped(flow)
    turned_shade = swapped(shade)
    sums = [
        jnp.sum(product, axis=0, keepdims=True)
        for product in (shade * own, turned_shade * own, shade * resid, turned_shade * resid)
    ]
    eight = lax.broadcasted_iota(jnp.int32, (8, 128), 0)
    stacked = jnp.zeros((8, 128), jnp.float32)
    for i, row in enumerate(sums):
        stacked = jnp.where(eight == i, row, stacked)
    stacked = fold(stacked)
    eight_group = lanes(8) // 16
    own_row = jnp.sum(jnp.where(eight_group == eight, stacked, 0.0), axis=0, keepdims=True)

    drain(1, tgt_all, D - 1)
    tgt_t[...] = tgt_all[...].reshape(T, 128).T
    drain(0, spot_all, Z - 1)

    def fill(j, carry):
        row = spot_all[j]
        sx, sy, sz = (
            jnp.sum(jnp.where((group == i) & diagonal, row, 0.0), axis=1, keepdims=True) for i in range(3)
        )
        place = pl.ds(pl.multiple_of(j * SH, SH), SH)
        for part in range(2):
            cols = slice(part * (T // 2), (part + 1) * (T // 2))
            tx, ty, tz = (tgt_t[PLANES + i : PLANES + i + 1, cols] for i in range(3))
            for which, value in enumerate(green(tx, ty, tz, sx, sy, sz)):
                high = value.astype(jnp.bfloat16)
                ghi[which, place, cols] = high
                glo[which, place, cols] = (value - high.astype(jnp.float32)).astype(jnp.bfloat16)
        return carry

    lax.fori_loop(0, Z, fill, 0)
    drain(2, src_all, Z - 1)

    flows = src_all[...].reshape(S, 128).T
    f_hi = flows.astype(jnp.bfloat16)
    f_lo = (flows - f_hi.astype(jnp.float32)).astype(jnp.bfloat16)

    def two(array, comp):
        return [rows(array, 0, comp), rows(array, 1, comp)]

    sums = [[0.0, 0.0, 0.0], [0.0, 0.0, 0.0]]
    for which, (a, b) in enumerate(PAIRS):
        high = two(f_hi, a) if a == b else two(f_hi, b) + two(f_hi, a)
        low = two(f_lo, a) if a == b else two(f_lo, b) + two(f_lo, a)
        height = 16 * len(high)
        both = jnp.concatenate(high + low, axis=0)
        high = both[:height]
        for part in range(2):
            one = jnp.dot(both, ghi[2 * which + part], preferred_element_type=jnp.float32)
            other = jnp.dot(high, glo[2 * which + part], preferred_element_type=jnp.float32)
            got = one[:height] + one[height:] + other
            sums[part][a] = sums[part][a] + got[:32]
            if a != b:
                sums[part][b] = sums[part][b] + got[32:]

    field_re = [sums[0][i][:16] - sums[1][i][16:] for i in range(3)]
    field_im = [sums[0][i][16:] + sums[1][i][:16] for i in range(3)]
    den_re = den_im = 0.0
    for i in range(3):
        sr, si = rows(tgt_t, 0, i), rows(tgt_t, 1, i)
        den_re = den_re + sr * field_re[i] + si * field_im[i]
        den_im = den_im + sr * field_im[i] - si * field_re[i]
    den_re = jnp.sum(den_re, axis=1, keepdims=True)
    den_im = jnp.sum(den_im, axis=1, keepdims=True)
    spread = jnp.where(group == 0, den_re, jnp.where(group == 1, den_im, 0.0))
    den_all[q] = own_row - jnp.sum(jnp.where(diagonal, spread, 0.0), axis=0, keepdims=True)

    def send_den(i, carry):
        copy(3, den_all.at[q], den_all.at[q], plane_peer(i)[1]).start()
        return carry

    def send_field(i, carry):
        other, device_id = plane_peer(i)
        copy(4, rs_send.at[other], rs_recv.at[q], device_id).start()
        return carry

    def send_fin(i, carry):
        copy(5, fin_all.at[z], fin_all.at[z], far_peer(i)).start()
        return carry

    lax.fori_loop(1, D, send_den, 0)
    partial = jnp.concatenate(field_re + field_im + [jnp.zeros((32, T), jnp.float32)], axis=0)
    rs_send[...] = partial.T.reshape(D, SH, 128)
    lax.fori_loop(1, D, send_field, 0)
    rs_recv[q] = rs_send[q]
    drain(3, den_all, D - 1)
    fin_all[z] = jnp.sum(den_all[...], axis=0)
    lax.fori_loop(1, Z, send_fin, 0)
    drain(4, rs_recv, D - 1)
    image = own - jnp.sum(rs_recv[...], axis=0)
    turned = swapped(image)
    img_out[...] = image[:, 0:PLANES]

    drain(5, fin_all, Z - 1)
    ends = jnp.sum(fin_all[...], axis=0)
    ends = fold(jnp.where(eight_group == eight, ends, 0.0))
    den_re, den_im, rho_re, rho_im = (ends[i : i + 1] for i in range(4))
    magnitude = jnp.maximum(den_re * den_re + den_im * den_im, 1.0)
    alpha_re = (rho_re * den_re + rho_im * den_im) / magnitude
    alpha_im = (rho_im * den_re - rho_re * den_im) / magnitude
    half_out[...] = (resid - (alpha_re * image + alpha_im * turned))[:, 0:PLANES]


def local(R, C, currents, residual, shadow, lattice_sites, classes, inverse_polarizability):
    f32 = jnp.float32
    Z, D = R // 2, 2 * C
    T, S = D * SH, Z * SH
    shape = jax.ShapeDtypeStruct((SH, PLANES), f32)
    image, half = pl.pallas_call(
        functools.partial(body, Z, C),
        out_shape=(shape, shape),
        in_specs=[pl.BlockSpec(memory_space=pltpu.HBM)] * 6,
        out_specs=(pl.BlockSpec(memory_space=pltpu.VMEM), pl.BlockSpec(memory_space=pltpu.VMEM)),
        scratch_shapes=[
            pltpu.VMEM((SH, PLANES), f32),
            pltpu.VMEM((SH, PLANES), f32),
            pltpu.VMEM((SH, PLANES), f32),
            pltpu.VMEM((3, SH), jnp.int32),
            pltpu.VMEM((1, SH), jnp.int32),
            pltpu.VMEM(inverse_polarizability.shape, f32),
            pltpu.VMEM((3, SH, 128), f32),
            pltpu.VMEM((Z, SH, 128), f32),
            pltpu.VMEM((Z, 1, 128), f32),
            pltpu.VMEM((D, SH, 128), f32),
            pltpu.VMEM((128, T), f32),
            pltpu.VMEM((12, S, T), jnp.bfloat16),
            pltpu.VMEM((12, S, T), jnp.bfloat16),
            pltpu.VMEM((D, SH, 128), f32),
            pltpu.VMEM((D, SH, 128), f32),
            pltpu.VMEM((D, 1, 128), f32),
            pltpu.VMEM((Z, 1, 128), f32),
            pltpu.SemaphoreType.DMA((6,)),
            pltpu.SemaphoreType.DMA((6,)),
            pltpu.SemaphoreType.DMA((6,)),
        ],
        compiler_params=pltpu.CompilerParams(
            collective_id=0, has_side_effects=True, vmem_limit_bytes=62 * 1024 * 1024
        ),
    )(currents.T, residual.T, shadow.T, lattice_sites, classes.reshape(1, SH), inverse_polarizability)
    return image.T, half.T


def solution(mesh):
    both = ("row", "col")
    in_specs = (P(None, both), P(None, both), P(None, both), P(None, both), P(both), P())
    out_specs = (P(None, both), P(None, both))
    step = functools.partial(local, mesh.shape["row"], mesh.shape["col"])
    return jax.shard_map(step, mesh=mesh, in_specs=in_specs, out_specs=out_specs, check_vma=False)
```

```python
import functools
import math

import jax
import jax.numpy as jnp
import numpy as np
from jax import lax
from jax.experimental import pallas as pl
from jax.experimental.pallas import tpu as pltpu
from jax.sharding import PartitionSpec as P

MESH = pl.DeviceIdType.MESH
K = 0.9
SH = 16
PLANES = 96
PAIRS = ((0, 0), (1, 1), (2, 2), (0, 1), (0, 2), (1, 2))


def _fit(terms, odd):
    nodes = 0.5 * np.cos((np.arange(400) + 0.5) * np.pi / 400)
    powers = np.arange(terms) * 2 + (1 if odd else 0)
    values = np.sin(2 * np.pi * nodes) if odd else np.cos(2 * np.pi * nodes)
    solved = np.linalg.lstsq(nodes[:, None] ** powers[None, :], values, rcond=None)[0]
    return [float(x) for x in solved]


SIN = _fit(6, True)
COS = _fit(7, False)


def _horner(coefs, x):
    out = jnp.float32(coefs[-1])
    for coef in coefs[-2::-1]:
        out = out * x + jnp.float32(coef)
    return out


def green(tx, ty, tz, sx, sy, sz):
    dx, dy, dz = tx - sx, ty - sy, tz - sz
    xx, yy, zz = dx * dx, dy * dy, dz * dz
    dist_sq = xx + yy + zz
    safe = jnp.maximum(dist_sq, 1.0)
    inv = lax.rsqrt(safe)
    dist = safe * inv
    reach = inv * jnp.minimum(dist_sq, 1.0)
    turns = dist * jnp.float32(K / (2 * math.pi))
    frac = turns - jnp.round(turns)
    frac_sq = frac * frac
    e_re = _horner(COS, frac_sq) * reach
    e_im = _horner(SIN, frac_sq) * frac * reach
    inv_sq = inv * inv
    iso_re = jnp.float32(K * K) - inv_sq
    iso_im = jnp.float32(K) * inv
    a_re = e_re * iso_re - e_im * iso_im
    a_im = e_im * iso_re + e_re * iso_im
    b_re = (jnp.float32(2 * K * K) * e_re - 3.0 * a_re) * inv_sq
    b_im = (jnp.float32(2 * K * K) * e_im - 3.0 * a_im) * inv_sq
    outer = (xx, yy, zz, dx * dy, dx * dz, dy * dz)
    parts = []
    for place, product in enumerate(outer):
        re, im = product * b_re, product * b_im
        if place < 3:
            re, im = re + a_re, im + a_im
        parts.extend((re, im))
    return parts


def rows(array, b, component):
    start = b * 48 + component * 16
    return array[start : start + 16]


def lanes(height):
    return lax.broadcasted_iota(jnp.int32, (height, 128), 1)


def sublanes(height):
    return lax.broadcasted_iota(jnp.int32, (height, 128), 0)


def swapped(block):
    lane = lanes(block.shape[0])
    turned = jnp.where(lane < 48, -pltpu.roll(block, 80, 1), pltpu.roll(block, 48, 1))
    return jnp.where(lane < PLANES, turned, 0.0)


def fold(block):
    for shift in (64, 32, 16):
        block = block + pltpu.roll(block, shift, 1)
    return block


def body(
    Z, C,
    cur_hbm, res_hbm, sha_hbm, site_hbm, cls_hbm, pol_hbm,
    img_out, half_out,
    cur, res, sha, site, cls, pol,
    wide, src_all, spot_all, here_all, axes_t, axes_s, tgt_all, tgt_t, fields, ghi, glo, rs_send, rs_recv, den_all, fin_all,
    in_sems, send_sems, recv_sems,
):
    r, c = lax.axis_index("row"), lax.axis_index("col")
    z, core = r // 2, r % 2
    D = 2 * C
    q = core * C + c
    T, S = D * SH, Z * SH

    def wrap(i, size):
        return jnp.where(i >= size, i - size, i)

    def plane_peer(i):
        other = wrap(q + i, D)
        upper = other >= C
        return other, {"row": z * 2 + jnp.where(upper, 1, 0), "col": jnp.where(upper, other - C, other)}

    HALF, OWN = Z // 2, Z // 4

    def far_peer(i):
        step = jnp.where(i % 2 == 0, HALF + i // 2, HALF - i // 2)
        return wrap(OWN - step + Z, Z), {"row": wrap(z + step, Z) * 2 + core}

    pairs = ((cur_hbm, cur), (res_hbm, res), (sha_hbm, sha), (site_hbm, site), (cls_hbm, cls), (pol_hbm, pol))
    loads = [pltpu.make_async_copy(a, b, in_sems.at[i]) for i, (a, b) in enumerate(pairs)]
    for load in loads:
        load.start()

    barrier = pltpu.get_barrier_semaphore()

    def greet_far(i, carry):
        pl.semaphore_signal(barrier, inc=1, device_id=far_peer(i)[1], device_id_type=MESH)
        return carry

    def greet_plane(i, carry):
        pl.semaphore_signal(barrier, inc=1, device_id=plane_peer(i)[1], device_id_type=MESH)
        return carry

    lax.fori_loop(1, Z, greet_far, 0)
    lax.fori_loop(1, D, greet_plane, 0)

    wide[...] = jnp.zeros_like(wide)
    for load in loads:
        load.wait()

    for i, ref in enumerate((cur, res, sha)):
        wide[i, :, 0:PLANES] = ref[...]
    lane, sublane = lanes(SH), sublanes(SH)
    group, diagonal = lane // 16, lane % 16 == sublane
    small_lane = lax.broadcasted_iota(jnp.int32, (SH, SH), 1)
    small_sublane = lax.broadcasted_iota(jnp.int32, (SH, SH), 0)

    def column(row):
        return jnp.sum(jnp.where(small_lane == small_sublane, row, 0.0), axis=1, keepdims=True)

    flow, resid, shade = wide[0], wide[1], wide[2]
    spots = site[...].astype(jnp.float32)
    axes = [column(spots[i : i + 1]) for i in range(3)]
    block = shade
    spot_row = jnp.zeros((SH, 128), jnp.float32)
    for i in range(3):
        block = jnp.where(lane == PLANES + i, axes[i], block)
        spot_row = jnp.where((group == i) & diagonal, axes[i], spot_row)
    tgt_all[q] = block
    spot_row = jnp.sum(spot_row, axis=0, keepdims=True)
    spot_all[OWN] = spot_row
    here_all[q] = spot_row
    src_all[OWN] = flow

    def copy(which, src, dst, device_id):
        return pltpu.make_async_remote_copy(
            src_ref=src, dst_ref=dst, send_sem=send_sems.at[which], recv_sem=recv_sems.at[which],
            device_id=device_id, device_id_type=MESH,
        )

    def send_here(i, carry):
        copy(0, here_all.at[q], here_all.at[q], plane_peer(i)[1]).start()
        return carry

    def send_spot(which, i, carry):
        slot, device_id = far_peer(i)
        copy(which, spot_all.at[OWN], spot_all.at[slot], device_id).start()
        return carry

    def send_src(which, i, carry):
        slot, device_id = far_peer(i)
        copy(which, src_all.at[OWN], src_all.at[slot], device_id).start()
        return carry

    def send_tgt(i, carry):
        copy(5, tgt_all.at[q], tgt_all.at[q], plane_peer(i)[1]).start()
        return carry

    def drain(which, buffer, count):
        whole = buffer.at[pl.ds(0, count)]
        copy(which, whole, whole, far_peer(1)[1]).wait()

    class_col = column(cls[...].astype(jnp.float32))
    pol_re = jnp.zeros((SH, 1), jnp.float32)
    pol_im = jnp.zeros((SH, 1), jnp.float32)
    for kind in range(pol.shape[1]):
        pol_re = jnp.where(class_col == kind, pol[0:1, kind : kind + 1], pol_re)
        pol_im = jnp.where(class_col == kind, pol[1:2, kind : kind + 1], pol_im)
    own = pol_re * flow + pol_im * swapped(flow)
    turned_shade = swapped(shade)
    sums = [
        jnp.sum(product, axis=0, keepdims=True)
        for product in (shade * own, turned_shade * own, shade * resid, turned_shade * resid)
    ]
    eight = lax.broadcasted_iota(jnp.int32, (8, 128), 0)
    stacked = jnp.zeros((8, 128), jnp.float32)
    for i, row in enumerate(sums):
        stacked = jnp.where(eight == i, row, stacked)
    stacked = fold(stacked)
    eight_group = lanes(8) // 16
    own_row = jnp.sum(jnp.where(eight_group == eight, stacked, 0.0), axis=0, keepdims=True)

    pl.semaphore_wait(barrier, Z + D - 2)
    lax.fori_loop(1, D, send_here, 0)
    lax.fori_loop(HALF + 1, Z, functools.partial(send_spot, 1), 0)
    lax.fori_loop(1, HALF + 1, functools.partial(send_spot, 2), 0)
    lax.fori_loop(1, HALF + 1, functools.partial(send_src, 3), 0)
    lax.fori_loop(HALF + 1, Z, functools.partial(send_src, 4), 0)
    lax.fori_loop(1, D, send_tgt, 0)

    drain(0, here_all, D - 1)
    for part in range(T // 128):
        eight_rows = here_all[part * 8 : part * 8 + 8].reshape(8, 128)
        for i in range(3):
            tiled = fold(jnp.where(eight_group == i, eight_rows, 0.0))
            picked = jnp.sum(jnp.where(eight_group == eight, tiled, 0.0), axis=0, keepdims=True)
            axes_t[i : i + 1, part * 128 : part * 128 + 128] = picked

    def spread_spots(j, carry):
        row = spot_all[j]
        for i in range(3):
            col = jnp.sum(jnp.where((group == i) & diagonal, row, 0.0), axis=1, keepdims=True)
            axes_s[i, pl.ds(pl.multiple_of(j * SH, SH), SH), :] = jnp.broadcast_to(col, (SH, 128))
        return carry

    def fill(j, carry):
        place = pl.ds(pl.multiple_of(j * SH, SH), SH)
        wide_t = T // 2
        sx, sy, sz = (jnp.tile(axes_s[i, place, :], (1, wide_t // 128)) for i in range(3))
        for part in range(2):
            cols = slice(part * wide_t, (part + 1) * wide_t)
            tx, ty, tz = (axes_t[i : i + 1, cols] for i in range(3))
            for which, value in enumerate(green(tx, ty, tz, sx, sy, sz)):
                high = value.astype(jnp.bfloat16)
                ghi[which, place, cols] = high
                glo[which, place, cols] = (value - high.astype(jnp.float32)).astype(jnp.bfloat16)
        return carry

    def two(array, comp):
        return [rows(array, 0, comp), rows(array, 1, comp)]

    def products(part):
        span = slice(part * (S // 2), (part + 1) * (S // 2))
        flows = src_all[part * HALF : (part + 1) * HALF].reshape(S // 2, 128).T
        f_hi = flows.astype(jnp.bfloat16)
        f_lo = (flows - f_hi.astype(jnp.float32)).astype(jnp.bfloat16)
        sums = [[0.0, 0.0, 0.0], [0.0, 0.0, 0.0]]
        for which, (a, b) in enumerate(PAIRS):
            high = two(f_hi, a) if a == b else two(f_hi, b) + two(f_hi, a)
            low = two(f_lo, a) if a == b else two(f_lo, b) + two(f_lo, a)
            height = 16 * len(high)
            both = jnp.concatenate(high + low, axis=0)
            high = both[:height]
            for ri in range(2):
                one = jnp.dot(both, ghi[2 * which + ri, span, :], preferred_element_type=jnp.float32)
                other = jnp.dot(high, glo[2 * which + ri, span, :], preferred_element_type=jnp.float32)
                got = one[:height] + one[height:] + other
                sums[ri][a] = sums[ri][a] + got[:32]
                if a != b:
                    sums[ri][b] = sums[ri][b] + got[32:]
        field_re = [sums[0][i][:16] - sums[1][i][16:] for i in range(3)]
        field_im = [sums[0][i][16:] + sums[1][i][:16] for i in range(3)]
        return field_re + field_im

    drain(1, spot_all, Z - 1 - HALF)
    lax.fori_loop(0, HALF, spread_spots, 0, unroll=True)
    lax.fori_loop(0, HALF, fill, 0)
    drain(2, spot_all, HALF)
    lax.fori_loop(HALF, Z, spread_spots, 0, unroll=True)
    lax.fori_loop(HALF, Z, fill, 0)
    drain(4, src_all, Z - 1 - HALF)
    fields[0:PLANES, :] = jnp.concatenate(products(0), axis=0)
    fields[PLANES:128, :] = jnp.zeros((128 - PLANES, T), jnp.float32)
    drain(5, tgt_all, D - 1)
    tgt_t[...] = tgt_all[...].reshape(T, 128).T
    drain(3, src_all, HALF)
    parts = products(1)
    den_re = den_im = 0.0
    for i in range(3):
        sr, si = rows(tgt_t, 0, i), rows(tgt_t, 1, i)
        re, im = rows(fields, 0, i) + parts[i], rows(fields, 1, i) + parts[3 + i]
        den_re = den_re + sr * re + si * im
        den_im = den_im + sr * im - si * re
        fields[i * 16 : i * 16 + 16, :] = re
        fields[48 + i * 16 : 64 + i * 16, :] = im
    den_re = jnp.sum(den_re, axis=1, keepdims=True)
    den_im = jnp.sum(den_im, axis=1, keepdims=True)
    spread = jnp.where(group == 0, den_re, jnp.where(group == 1, den_im, 0.0))
    den_all[q] = own_row - jnp.sum(jnp.where(diagonal, spread, 0.0), axis=0, keepdims=True)

    def send_den(i, carry):
        copy(6, den_all.at[q], den_all.at[q], plane_peer(i)[1]).start()
        return carry

    def send_field(i, carry):
        other, device_id = plane_peer(i)
        copy(7, rs_send.at[other], rs_recv.at[q], device_id).start()
        return carry

    def send_fin(i, carry):
        slot, device_id = far_peer(i)
        copy(8, fin_all.at[OWN], fin_all.at[slot], device_id).start()
        return carry

    lax.fori_loop(1, D, send_den, 0)
    rs_send[...] = fields[...].T.reshape(D, SH, 128)
    lax.fori_loop(1, D, send_field, 0)
    rs_recv[q] = rs_send[q]
    drain(6, den_all, D - 1)
    fin_all[OWN] = jnp.sum(den_all[...], axis=0)
    lax.fori_loop(1, Z, send_fin, 0)
    drain(7, rs_recv, D - 1)
    image = own - jnp.sum(rs_recv[...], axis=0)
    turned = swapped(image)
    img_out[...] = image[:, 0:PLANES]

    drain(8, fin_all, Z - 1)
    ends = jnp.sum(fin_all[...], axis=0)
    ends = fold(jnp.where(eight_group == eight, ends, 0.0))
    den_re, den_im, rho_re, rho_im = (ends[i : i + 1] for i in range(4))
    magnitude = jnp.maximum(den_re * den_re + den_im * den_im, 1.0)
    alpha_re = (rho_re * den_re + rho_im * den_im) / magnitude
    alpha_im = (rho_im * den_re - rho_re * den_im) / magnitude
    half_out[...] = (resid - (alpha_re * image + alpha_im * turned))[:, 0:PLANES]


def deliver(image, half, image_out, half_out, sems):
    copies = [pltpu.make_async_copy(image, image_out, sems.at[0]), pltpu.make_async_copy(half, half_out, sems.at[1])]
    for one in copies:
        one.start()
    for one in copies:
        one.wait()


def local(R, C, currents, residual, shadow, lattice_sites, classes, inverse_polarizability):
    f32 = jnp.float32
    Z, D = R // 2, 2 * C
    T, S = D * SH, Z * SH
    shape = jax.ShapeDtypeStruct((SH, PLANES), f32)
    blocks = pl.pallas_call(
        functools.partial(body, Z, C),
        out_shape=(pltpu.VMEM((SH, PLANES), f32), pltpu.VMEM((SH, PLANES), f32)),
        in_specs=[pl.BlockSpec(memory_space=pltpu.HBM)] * 6,
        out_specs=(pl.BlockSpec(memory_space=pltpu.VMEM), pl.BlockSpec(memory_space=pltpu.VMEM)),
        scratch_shapes=[
            pltpu.VMEM((SH, PLANES), f32),
            pltpu.VMEM((SH, PLANES), f32),
            pltpu.VMEM((SH, PLANES), f32),
            pltpu.VMEM((3, SH), jnp.int32),
            pltpu.VMEM((1, SH), jnp.int32),
            pltpu.VMEM(inverse_polarizability.shape, f32),
            pltpu.VMEM((3, SH, 128), f32),
            pltpu.VMEM((Z, SH, 128), f32),
            pltpu.VMEM((Z, 1, 128), f32),
            pltpu.VMEM((D, 1, 128), f32),
            pltpu.VMEM((8, T), f32),
            pltpu.VMEM((3, S, 128), f32),
            pltpu.VMEM((D, SH, 128), f32),
            pltpu.VMEM((128, T), f32),
            pltpu.VMEM((128, T), f32),
            pltpu.VMEM((12, S, T), jnp.bfloat16),
            pltpu.VMEM((12, S, T), jnp.bfloat16),
            pltpu.VMEM((D, SH, 128), f32),
            pltpu.VMEM((D, SH, 128), f32),
            pltpu.VMEM((D, 1, 128), f32),
            pltpu.VMEM((Z, 1, 128), f32),
            pltpu.SemaphoreType.DMA((6,)),
            pltpu.SemaphoreType.DMA((9,)),
            pltpu.SemaphoreType.DMA((9,)),
        ],
        compiler_params=pltpu.CompilerParams(
            collective_id=0, has_side_effects=True, vmem_limit_bytes=62 * 1024 * 1024
        ),
    )(currents.T, residual.T, shadow.T, lattice_sites, classes.reshape(1, SH), inverse_polarizability)
    image, half = pl.pallas_call(
        deliver,
        out_shape=(shape, shape),
        in_specs=[pl.BlockSpec(memory_space=pltpu.VMEM)] * 2,
        out_specs=(pl.BlockSpec(memory_space=pltpu.HBM), pl.BlockSpec(memory_space=pltpu.HBM)),
        scratch_shapes=[pltpu.SemaphoreType.DMA((2,))],
    )(*(pltpu.with_memory_space_constraint(block, pltpu.VMEM) for block in blocks))
    return image.T, half.T


def solution(mesh):
    both = ("row", "col")
    in_specs = (P(None, both), P(None, both), P(None, both), P(None, both), P(both), P())
    out_specs = (P(None, both), P(None, both))
    step = functools.partial(local, mesh.shape["row"], mesh.shape["col"])
    return jax.shard_map(step, mesh=mesh, in_specs=in_specs, out_specs=out_specs, check_vma=False)
```

```python
import functools
import math

import jax
import jax.numpy as jnp
import numpy as np
from jax import lax
from jax.experimental import pallas as pl
from jax.experimental.pallas import tpu as pltpu
from jax.sharding import PartitionSpec as P

MESH = pl.DeviceIdType.MESH
K = 0.9
SH = 16
PLANES = 96
PAIRS = ((0, 0), (1, 1), (2, 2), (0, 1), (0, 2), (1, 2))


def _fit(terms, odd):
    nodes = 0.5 * np.cos((np.arange(400) + 0.5) * np.pi / 400)
    powers = np.arange(terms) * 2 + (1 if odd else 0)
    values = np.sin(2 * np.pi * nodes) if odd else np.cos(2 * np.pi * nodes)
    solved = np.linalg.lstsq(nodes[:, None] ** powers[None, :], values, rcond=None)[0]
    return [float(x) for x in solved]


SIN = _fit(6, True)
COS = _fit(7, False)


def _horner(coefs, x):
    out = jnp.float32(coefs[-1])
    for coef in coefs[-2::-1]:
        out = out * x + jnp.float32(coef)
    return out


def green(tx, ty, tz, sx, sy, sz):
    dx, dy, dz = tx - sx, ty - sy, tz - sz
    xx, yy, zz = dx * dx, dy * dy, dz * dz
    dist_sq = xx + yy + zz
    safe = jnp.maximum(dist_sq, 1.0)
    inv = lax.rsqrt(safe)
    dist = safe * inv
    reach = inv * jnp.minimum(dist_sq, 1.0)
    turns = dist * jnp.float32(K / (2 * math.pi))
    frac = turns - jnp.round(turns)
    frac_sq = frac * frac
    e_re = _horner(COS, frac_sq) * reach
    e_im = _horner(SIN, frac_sq) * frac * reach
    inv_sq = inv * inv
    iso_re = jnp.float32(K * K) - inv_sq
    iso_im = jnp.float32(K) * inv
    a_re = e_re * iso_re - e_im * iso_im
    a_im = e_im * iso_re + e_re * iso_im
    b_re = (jnp.float32(2 * K * K) * e_re - 3.0 * a_re) * inv_sq
    b_im = (jnp.float32(2 * K * K) * e_im - 3.0 * a_im) * inv_sq
    outer = (xx, yy, zz, dx * dy, dx * dz, dy * dz)
    parts = []
    for place, product in enumerate(outer):
        re, im = product * b_re, product * b_im
        if place < 3:
            re, im = re + a_re, im + a_im
        parts.extend((re, im))
    return parts


def rows(array, b, component):
    start = b * 48 + component * 16
    return array[start : start + 16]


def lanes(height):
    return lax.broadcasted_iota(jnp.int32, (height, 128), 1)


def sublanes(height):
    return lax.broadcasted_iota(jnp.int32, (height, 128), 0)


def swapped(block):
    lane = lanes(block.shape[0])
    turned = jnp.where(lane < 48, -pltpu.roll(block, 80, 1), pltpu.roll(block, 48, 1))
    return jnp.where(lane < PLANES, turned, 0.0)


def fold(block):
    for shift in (64, 32, 16):
        block = block + pltpu.roll(block, shift, 1)
    return block


def body(
    Z, C,
    cur_hbm, res_hbm, sha_hbm, site_hbm, cls_hbm, pol_hbm,
    img_out, half_out,
    cur, res, sha, site, cls, pol,
    wide, src_all, spot_all, here_all, axes_t, axes_s, tgt_all, tgt_t, fields, ghi, glo, rs_send, rs_recv, den_all, fin_all,
    in_sems, send_sems, recv_sems,
):
    r, c = lax.axis_index("row"), lax.axis_index("col")
    z, core = r // 2, r % 2
    D = 2 * C
    q = core * C + c
    T, S = D * SH, Z * SH

    def wrap(i, size):
        return jnp.where(i >= size, i - size, i)

    def plane_peer(i):
        other = wrap(q + i, D)
        upper = other >= C
        return other, {"row": z * 2 + jnp.where(upper, 1, 0), "col": jnp.where(upper, other - C, other)}

    HALF, OWN = Z // 2, Z // 4
    LAST = 3 if Z > 4 else 1
    FIRST_LAST = OWN + HALF - LAST // 2

    def far_peer(i):
        step = jnp.where(i % 2 == 0, HALF + i // 2, HALF - i // 2)
        return wrap(OWN - step + Z, Z), {"row": wrap(z + step, Z) * 2 + core}

    def lead_peer(i, to_core):
        step = jnp.where(i % 2 == 0, HALF + i // 2, HALF - i // 2)
        return {"row": wrap(z + step, Z) * 2 + to_core}

    barrier = pltpu.get_barrier_semaphore()

    def greet_far(i, carry):
        pl.semaphore_signal(barrier, inc=1, device_id=far_peer(i)[1], device_id_type=MESH)
        return carry

    def greet_plane(i, carry):
        pl.semaphore_signal(barrier, inc=1, device_id=plane_peer(i)[1], device_id_type=MESH)
        return carry

    lax.fori_loop(1, Z, greet_far, 0)

    lax.fori_loop(1, D, greet_plane, 0)

    pairs = ((cur_hbm, cur), (res_hbm, res), (sha_hbm, sha), (site_hbm, site), (cls_hbm, cls), (pol_hbm, pol))
    loads = [pltpu.make_async_copy(a, b, in_sems.at[i]) for i, (a, b) in enumerate(pairs)]
    for load in loads:
        load.start()

    wide[...] = jnp.zeros_like(wide)
    for load in loads:
        load.wait()

    for i, ref in enumerate((cur, res, sha)):
        wide[i, :, 0:PLANES] = ref[...]
    lane, sublane = lanes(SH), sublanes(SH)
    group, diagonal = lane // 16, lane % 16 == sublane
    small_lane = lax.broadcasted_iota(jnp.int32, (SH, SH), 1)
    small_sublane = lax.broadcasted_iota(jnp.int32, (SH, SH), 0)

    def column(row):
        return jnp.sum(jnp.where(small_lane == small_sublane, row, 0.0), axis=1, keepdims=True)

    flow, resid, shade = wide[0], wide[1], wide[2]
    spots = site[...].astype(jnp.float32)
    axes = [column(spots[i : i + 1]) for i in range(3)]
    block = shade
    spot_row = jnp.zeros((SH, 128), jnp.float32)
    for i in range(3):
        block = jnp.where(lane == PLANES + i, axes[i], block)
        spot_row = jnp.where((group == i) & diagonal, axes[i], spot_row)
    tgt_all[q] = block
    spot_row = jnp.sum(spot_row, axis=0, keepdims=True)
    spot_all[OWN] = spot_row
    here_all[q] = spot_row
    src_all[OWN] = flow

    def copy(which, src, dst, device_id):
        return pltpu.make_async_remote_copy(
            src_ref=src, dst_ref=dst, send_sem=send_sems.at[which], recv_sem=recv_sems.at[which],
            device_id=device_id, device_id_type=MESH,
        )

    def send_here(i, carry):
        copy(0, here_all.at[q], here_all.at[q], plane_peer(i)[1]).start()
        return carry

    def send_spot(which, i, carry):
        slot, device_id = far_peer(i)
        copy(which, spot_all.at[OWN], spot_all.at[slot], device_id).start()
        return carry

    def send_src(which, i, carry):
        slot, device_id = far_peer(i)
        copy(which, src_all.at[OWN], src_all.at[slot], device_id).start()
        return carry

    def send_tgt(i, carry):
        copy(5, tgt_all.at[q], tgt_all.at[q], plane_peer(i)[1]).start()
        return carry

    def drain(which, buffer, count):
        whole = buffer.at[pl.ds(0, count)]
        copy(which, whole, whole, far_peer(1)[1]).wait()

    class_col = column(cls[...].astype(jnp.float32))
    pol_re = jnp.zeros((SH, 1), jnp.float32)
    pol_im = jnp.zeros((SH, 1), jnp.float32)
    for kind in range(pol.shape[1]):
        pol_re = jnp.where(class_col == kind, pol[0:1, kind : kind + 1], pol_re)
        pol_im = jnp.where(class_col == kind, pol[1:2, kind : kind + 1], pol_im)
    own = pol_re * flow + pol_im * swapped(flow)
    turned_shade = swapped(shade)
    sums = [
        jnp.sum(product, axis=0, keepdims=True)
        for product in (shade * own, turned_shade * own, shade * resid, turned_shade * resid)
    ]
    eight = lax.broadcasted_iota(jnp.int32, (8, 128), 0)
    stacked = jnp.zeros((8, 128), jnp.float32)
    for i, row in enumerate(sums):
        stacked = jnp.where(eight == i, row, stacked)
    stacked = fold(stacked)
    eight_group = lanes(8) // 16
    own_row = jnp.sum(jnp.where(eight_group == eight, stacked, 0.0), axis=0, keepdims=True)


    pl.semaphore_wait(barrier, Z + D - 2)
    @pl.when(z < HALF)
    def _():
        lax.fori_loop(1, LAST + 1, functools.partial(send_spot, 2), 0, unroll=True)
        lax.fori_loop(LAST + 1, HALF + 1, functools.partial(send_spot, 9), 0, unroll=True)
        lax.fori_loop(1, HALF + 1, functools.partial(send_src, 3), 0, unroll=True)
        lax.fori_loop(1, D, send_here, 0, unroll=True)
        lax.fori_loop(HALF + 1, Z, functools.partial(send_spot, 1), 0, unroll=True)

    @pl.when(z >= HALF)
    def _():
        lax.fori_loop(1, D, send_here, 0, unroll=True)
        lax.fori_loop(HALF + 1, Z, functools.partial(send_spot, 1), 0, unroll=True)
        lax.fori_loop(1, LAST + 1, functools.partial(send_spot, 2), 0, unroll=True)
        lax.fori_loop(LAST + 1, HALF + 1, functools.partial(send_spot, 9), 0, unroll=True)
        lax.fori_loop(1, HALF + 1, functools.partial(send_src, 3), 0, unroll=True)

    lax.fori_loop(HALF + 1, Z, functools.partial(send_src, 4), 0, unroll=True)
    lax.fori_loop(1, D, send_tgt, 0, unroll=True)

    drain(0, here_all, D - 1)
    for part in range(T // 128):
        eight_rows = here_all[part * 8 : part * 8 + 8].reshape(8, 128)
        for i in range(3):
            tiled = fold(jnp.where(eight_group == i, eight_rows, 0.0))
            picked = jnp.sum(jnp.where(eight_group == eight, tiled, 0.0), axis=0, keepdims=True)
            axes_t[i : i + 1, part * 128 : part * 128 + 128] = picked

    def spread_spots(j, carry):
        row = spot_all[j]
        for i in range(3):
            col = jnp.sum(jnp.where((group == i) & diagonal, row, 0.0), axis=1, keepdims=True)
            axes_s[i, pl.ds(pl.multiple_of(j * SH, SH), SH), :] = jnp.broadcast_to(col, (SH, 128))
        return carry

    def fill(j, carry):
        place = pl.ds(pl.multiple_of(j * SH, SH), SH)
        wide_t = T // 2
        sx, sy, sz = (jnp.tile(axes_s[i, place, :], (1, wide_t // 128)) for i in range(3))
        for part in range(2):
            cols = slice(part * wide_t, (part + 1) * wide_t)
            tx, ty, tz = (axes_t[i : i + 1, cols] for i in range(3))
            for which, value in enumerate(green(tx, ty, tz, sx, sy, sz)):
                high = value.astype(jnp.bfloat16)
                ghi[which, place, cols] = high
                glo[which, place, cols] = (value - high.astype(jnp.float32)).astype(jnp.bfloat16)
        return carry

    def two(array, comp):
        return [rows(array, 0, comp), rows(array, 1, comp)]

    def products(part):
        span = slice(part * (S // 2), (part + 1) * (S // 2))
        flows = src_all[part * HALF : (part + 1) * HALF].reshape(S // 2, 128).T
        f_hi = flows.astype(jnp.bfloat16)
        f_lo = (flows - f_hi.astype(jnp.float32)).astype(jnp.bfloat16)
        sums = [[0.0, 0.0, 0.0], [0.0, 0.0, 0.0]]
        for which, (a, b) in enumerate(PAIRS):
            high = two(f_hi, a) if a == b else two(f_hi, b) + two(f_hi, a)
            low = two(f_lo, a) if a == b else two(f_lo, b) + two(f_lo, a)
            height = 16 * len(high)
            both = jnp.concatenate(high + low, axis=0)
            high = both[:height]
            for ri in range(2):
                one = jnp.dot(both, ghi[2 * which + ri, span, :], preferred_element_type=jnp.float32)
                other = jnp.dot(high, glo[2 * which + ri, span, :], preferred_element_type=jnp.float32)
                got = one[:height] + one[height:] + other
                sums[ri][a] = sums[ri][a] + got[:32]
                if a != b:
                    sums[ri][b] = sums[ri][b] + got[32:]
        field_re = [sums[0][i][:16] - sums[1][i][16:] for i in range(3)]
        field_im = [sums[0][i][16:] + sums[1][i][:16] for i in range(3)]
        return field_re + field_im

    drain(1, spot_all, Z - 1 - HALF)
    lax.fori_loop(0, HALF, spread_spots, 0, unroll=True)
    lax.fori_loop(0, HALF, fill, 0)
    drain(9, spot_all, HALF - LAST)
    for first, end in ((HALF, FIRST_LAST), (FIRST_LAST + LAST, Z)):
        lax.fori_loop(first, end, spread_spots, 0, unroll=True)
        lax.fori_loop(first, end, fill, 0)
    drain(4, src_all, Z - 1 - HALF)
    fields[0:PLANES, :] = jnp.concatenate(products(0), axis=0)
    fields[PLANES:128, :] = jnp.zeros((128 - PLANES, T), jnp.float32)
    drain(2, spot_all, LAST)
    lax.fori_loop(FIRST_LAST, FIRST_LAST + LAST, spread_spots, 0, unroll=True)
    lax.fori_loop(FIRST_LAST, FIRST_LAST + LAST, fill, 0)
    drain(5, tgt_all, D - 1)
    tgt_t[...] = tgt_all[...].reshape(T, 128).T
    drain(3, src_all, HALF)
    parts = products(1)
    den_re = den_im = 0.0
    for i in range(3):
        sr, si = rows(tgt_t, 0, i), rows(tgt_t, 1, i)
        re, im = rows(fields, 0, i) + parts[i], rows(fields, 1, i) + parts[3 + i]
        den_re = den_re + sr * re + si * im
        den_im = den_im + sr * im - si * re
        fields[i * 16 : i * 16 + 16, :] = re
        fields[48 + i * 16 : 64 + i * 16, :] = im
    den_re = jnp.sum(den_re, axis=1, keepdims=True)
    den_im = jnp.sum(den_im, axis=1, keepdims=True)
    spread = jnp.where(group == 0, den_re, jnp.where(group == 1, den_im, 0.0))
    den_all[q] = own_row - jnp.sum(jnp.where(diagonal, spread, 0.0), axis=0, keepdims=True)

    def send_den(i, carry):
        copy(6, den_all.at[q], den_all.at[q], {"row": z * 2 + 1, "col": wrap(c + i, C)}).start()
        return carry

    def send_field(i, carry):
        other, device_id = plane_peer(i)
        copy(7, rs_send.at[other], rs_recv.at[q], device_id).start()
        return carry

    def send_fin(to_core, i, carry):
        slot = far_peer(i)[0]
        copy(8, fin_all.at[OWN], fin_all.at[slot], lead_peer(i, to_core)).start()
        return carry

    def of(which, buffer, count):
        whole = buffer.at[pl.ds(0, count)]
        return copy(which, whole, whole, far_peer(1)[1])

    @pl.when(core == 0)
    def _():
        lax.fori_loop(0, C, send_den, 0)

    @pl.when(core == 1)
    def _():
        lax.fori_loop(1, C, send_den, 0)

    rs_send[...] = fields[...].T.reshape(D, SH, 128)
    lax.fori_loop(1, D, send_field, 0)
    rs_recv[q] = rs_send[q]

    @pl.when(core == 1)
    def _():
        of(6, den_all, D - 1).wait_recv()
        fin_all[OWN] = jnp.sum(den_all[...], axis=0)
        lax.fori_loop(1, Z, functools.partial(send_fin, 1), 0)
        lax.fori_loop(1, Z, functools.partial(send_fin, 0), 0)
        copy(8, fin_all.at[OWN], fin_all.at[OWN], {"row": z * 2}).start()

    drain(7, rs_recv, D - 1)
    image = own - jnp.sum(rs_recv[...], axis=0)
    turned = swapped(image)
    img_out[...] = image[:, 0:PLANES]

    @pl.when(core == 0)
    def _():
        of(6, den_all, C).wait_send()
        of(8, fin_all, Z).wait_recv()

    @pl.when(core == 1)
    def _():
        of(6, den_all, C - 1).wait_send()
        of(8, den_all, 2 * Z - 1).wait_send()
        of(8, fin_all, Z - 1).wait_recv()

    ends = jnp.sum(fin_all[...], axis=0)
    ends = fold(jnp.where(eight_group == eight, ends, 0.0))
    den_re, den_im, rho_re, rho_im = (ends[i : i + 1] for i in range(4))
    magnitude = jnp.maximum(den_re * den_re + den_im * den_im, 1.0)
    alpha_re = (rho_re * den_re + rho_im * den_im) / magnitude
    alpha_im = (rho_im * den_re - rho_re * den_im) / magnitude
    half_out[...] = (resid - (alpha_re * image + alpha_im * turned))[:, 0:PLANES]


def deliver(image, half, image_out, half_out, sems):
    copies = [pltpu.make_async_copy(image, image_out, sems.at[0]), pltpu.make_async_copy(half, half_out, sems.at[1])]
    for one in copies:
        one.start()
    for one in copies:
        one.wait()


def local(R, C, currents, residual, shadow, lattice_sites, classes, inverse_polarizability):
    f32 = jnp.float32
    Z, D = R // 2, 2 * C
    T, S = D * SH, Z * SH
    shape = jax.ShapeDtypeStruct((SH, PLANES), f32)
    blocks = pl.pallas_call(
        functools.partial(body, Z, C),
        out_shape=(pltpu.VMEM((SH, PLANES), f32), pltpu.VMEM((SH, PLANES), f32)),
        in_specs=[pl.BlockSpec(memory_space=pltpu.HBM)] * 6,
        out_specs=(pl.BlockSpec(memory_space=pltpu.VMEM), pl.BlockSpec(memory_space=pltpu.VMEM)),
        scratch_shapes=[
            pltpu.VMEM((SH, PLANES), f32),
            pltpu.VMEM((SH, PLANES), f32),
            pltpu.VMEM((SH, PLANES), f32),
            pltpu.VMEM((3, SH), jnp.int32),
            pltpu.VMEM((1, SH), jnp.int32),
            pltpu.VMEM(inverse_polarizability.shape, f32),
            pltpu.VMEM((3, SH, 128), f32),
            pltpu.VMEM((Z, SH, 128), f32),
            pltpu.VMEM((Z, 1, 128), f32),
            pltpu.VMEM((D, 1, 128), f32),
            pltpu.VMEM((8, T), f32),
            pltpu.VMEM((3, S, 128), f32),
            pltpu.VMEM((D, SH, 128), f32),
            pltpu.VMEM((128, T), f32),
            pltpu.VMEM((128, T), f32),
            pltpu.VMEM((12, S, T), jnp.bfloat16),
            pltpu.VMEM((12, S, T), jnp.bfloat16),
            pltpu.VMEM((D, SH, 128), f32),
            pltpu.VMEM((D, SH, 128), f32),
            pltpu.VMEM((D, 1, 128), f32),
            pltpu.VMEM((Z, 1, 128), f32),
            pltpu.SemaphoreType.DMA((6,)),
            pltpu.SemaphoreType.DMA((10,)),
            pltpu.SemaphoreType.DMA((10,)),
        ],
        compiler_params=pltpu.CompilerParams(
            collective_id=0, has_side_effects=True, vmem_limit_bytes=62 * 1024 * 1024
        ),
    )(currents.T, residual.T, shadow.T, lattice_sites, classes.reshape(1, SH), inverse_polarizability)
    image, half = pl.pallas_call(
        deliver,
        out_shape=(shape, shape),
        in_specs=[pl.BlockSpec(memory_space=pltpu.VMEM)] * 2,
        out_specs=(pl.BlockSpec(memory_space=pltpu.HBM), pl.BlockSpec(memory_space=pltpu.HBM)),
        scratch_shapes=[pltpu.SemaphoreType.DMA((2,))],
    )(*(pltpu.with_memory_space_constraint(block, pltpu.VMEM) for block in blocks))
    return image.T, half.T


def solution(mesh):
    both = ("row", "col")
    in_specs = (P(None, both), P(None, both), P(None, both), P(None, both), P(both), P())
    out_specs = (P(None, both), P(None, both))
    step = functools.partial(local, mesh.shape["row"], mesh.shape["col"])
    return jax.shard_map(step, mesh=mesh, in_specs=in_specs, out_specs=out_specs, check_vma=False)
```

```python
import functools
import math

import jax
import jax.numpy as jnp
import numpy as np
from jax import lax
from jax.experimental import pallas as pl
from jax.experimental.pallas import tpu as pltpu
from jax.sharding import PartitionSpec as P

MESH = pl.DeviceIdType.MESH
K = 0.9
SH = 16
PLANES = 96
PAIRS = ((0, 0), (1, 1), (2, 2), (0, 1), (0, 2), (1, 2))


def _fit(terms, odd):
    nodes = 0.5 * np.cos((np.arange(400) + 0.5) * np.pi / 400)
    powers = np.arange(terms) * 2 + (1 if odd else 0)
    values = np.sin(2 * np.pi * nodes) if odd else np.cos(2 * np.pi * nodes)
    solved = np.linalg.lstsq(nodes[:, None] ** powers[None, :], values, rcond=None)[0]
    return [float(x) for x in solved]


SIN = _fit(6, True)
COS = _fit(7, False)


def _horner(coefs, x):
    out = jnp.float32(coefs[-1])
    for coef in coefs[-2::-1]:
        out = out * x + jnp.float32(coef)
    return out


def green(tx, ty, tz, sx, sy, sz):
    dx, dy, dz = tx - sx, ty - sy, tz - sz
    xx, yy, zz = dx * dx, dy * dy, dz * dz
    dist_sq = xx + yy + zz
    safe = jnp.maximum(dist_sq, 1.0)
    inv = lax.rsqrt(safe)
    dist = safe * inv
    reach = inv * jnp.minimum(dist_sq, 1.0)
    turns = dist * jnp.float32(K / (2 * math.pi))
    frac = turns - jnp.round(turns)
    frac_sq = frac * frac
    e_re = _horner(COS, frac_sq) * reach
    e_im = _horner(SIN, frac_sq) * frac * reach
    inv_sq = inv * inv
    iso_re = jnp.float32(K * K) - inv_sq
    iso_im = jnp.float32(K) * inv
    a_re = e_re * iso_re - e_im * iso_im
    a_im = e_im * iso_re + e_re * iso_im
    b_re = (jnp.float32(2 * K * K) * e_re - 3.0 * a_re) * inv_sq
    b_im = (jnp.float32(2 * K * K) * e_im - 3.0 * a_im) * inv_sq
    outer = (xx, yy, zz, dx * dy, dx * dz, dy * dz)
    parts = []
    for place, product in enumerate(outer):
        re, im = product * b_re, product * b_im
        if place < 3:
            re, im = re + a_re, im + a_im
        parts.extend((re, im))
    return parts


def rows(array, b, component):
    start = b * 48 + component * 16
    return array[start : start + 16]


def lanes(height):
    return lax.broadcasted_iota(jnp.int32, (height, 128), 1)


def sublanes(height):
    return lax.broadcasted_iota(jnp.int32, (height, 128), 0)


def swapped(block):
    lane = lanes(block.shape[0])
    turned = jnp.where(lane < 48, -pltpu.roll(block, 80, 1), pltpu.roll(block, 48, 1))
    return jnp.where(lane < PLANES, turned, 0.0)


def fold(block):
    for shift in (64, 32, 16):
        block = block + pltpu.roll(block, shift, 1)
    return block


def body(
    Z, C,
    cur_hbm, res_hbm, sha_hbm, site_hbm, cls_hbm, pol_hbm,
    img_out, half_out,
    cur, res, sha, site, cls, pol,
    wide, src_all, spot_all, here_all, axes_t, axes_s, tgt_all, tgt_t, fields, ghi, glo, rs_send, rs_recv, den_all, fin_all, every, total,
    in_sems, send_sems, recv_sems,
):
    r, c = lax.axis_index("row"), lax.axis_index("col")
    z, core = r // 2, r % 2
    D = 2 * C
    q = core * C + c
    T, S = D * SH, Z * SH

    def wrap(i, size):
        return jnp.where(i >= size, i - size, i)

    def plane_peer(i):
        other = wrap(q + i, D)
        upper = other >= C
        return other, {"row": z * 2 + jnp.where(upper, 1, 0), "col": jnp.where(upper, other - C, other)}

    HALF, OWN = Z // 2, Z // 4
    LAST = 3 if Z > 4 else 1
    FIRST_LAST = OWN + HALF - LAST // 2

    def far_peer(i):
        step = jnp.where(i % 2 == 0, HALF + i // 2, HALF - i // 2)
        return wrap(OWN - step + Z, Z), {"row": wrap(z + step, Z) * 2 + core}

    def lead_peer(i, to_core):
        step = jnp.where(i % 2 == 0, HALF + i // 2, HALF - i // 2)
        return {"row": wrap(z + step, Z) * 2 + to_core}

    barrier = pltpu.get_barrier_semaphore()

    def greet_far(i, carry):
        pl.semaphore_signal(barrier, inc=1, device_id=far_peer(i)[1], device_id_type=MESH)
        return carry

    def greet_plane(i, carry):
        pl.semaphore_signal(barrier, inc=1, device_id=plane_peer(i)[1], device_id_type=MESH)
        return carry

    lax.fori_loop(1, Z, greet_far, 0)

    lax.fori_loop(1, D, greet_plane, 0)

    pairs = ((cur_hbm, cur), (res_hbm, res), (sha_hbm, sha), (site_hbm, site), (cls_hbm, cls), (pol_hbm, pol))
    loads = [pltpu.make_async_copy(a, b, in_sems.at[i]) for i, (a, b) in enumerate(pairs)]
    for load in loads:
        load.start()

    wide[...] = jnp.zeros_like(wide)
    for load in loads:
        load.wait()

    for i, ref in enumerate((cur, res, sha)):
        wide[i, :, 0:PLANES] = ref[...]
    lane, sublane = lanes(SH), sublanes(SH)
    group, diagonal = lane // 16, lane % 16 == sublane
    small_lane = lax.broadcasted_iota(jnp.int32, (SH, SH), 1)
    small_sublane = lax.broadcasted_iota(jnp.int32, (SH, SH), 0)

    def column(row):
        return jnp.sum(jnp.where(small_lane == small_sublane, row, 0.0), axis=1, keepdims=True)

    flow, resid, shade = wide[0], wide[1], wide[2]
    spots = site[...].astype(jnp.float32)
    axes = [column(spots[i : i + 1]) for i in range(3)]
    block = shade
    spot_row = jnp.zeros((SH, 128), jnp.float32)
    for i in range(3):
        block = jnp.where(lane == PLANES + i, axes[i], block)
        spot_row = jnp.where((group == i) & diagonal, axes[i], spot_row)
    tgt_all[q] = block
    spot_row = jnp.sum(spot_row, axis=0, keepdims=True)
    spot_all[OWN] = spot_row
    here_all[q] = spot_row
    src_all[OWN] = flow

    def copy(which, src, dst, device_id):
        return pltpu.make_async_remote_copy(
            src_ref=src, dst_ref=dst, send_sem=send_sems.at[which], recv_sem=recv_sems.at[which],
            device_id=device_id, device_id_type=MESH,
        )

    def send_here(i, carry):
        copy(0, here_all.at[q], here_all.at[q], plane_peer(i)[1]).start()
        return carry

    def send_spot(which, i, carry):
        slot, device_id = far_peer(i)
        copy(which, spot_all.at[OWN], spot_all.at[slot], device_id).start()
        return carry

    def send_src(which, i, carry):
        slot, device_id = far_peer(i)
        copy(which, src_all.at[OWN], src_all.at[slot], device_id).start()
        return carry

    def send_tgt(i, carry):
        copy(5, tgt_all.at[q], tgt_all.at[q], plane_peer(i)[1]).start()
        return carry

    def drain(which, buffer, count):
        whole = buffer.at[pl.ds(0, count)]
        copy(which, whole, whole, far_peer(1)[1]).wait()

    class_col = column(cls[...].astype(jnp.float32))
    pol_re = jnp.zeros((SH, 1), jnp.float32)
    pol_im = jnp.zeros((SH, 1), jnp.float32)
    for kind in range(pol.shape[1]):
        pol_re = jnp.where(class_col == kind, pol[0:1, kind : kind + 1], pol_re)
        pol_im = jnp.where(class_col == kind, pol[1:2, kind : kind + 1], pol_im)
    own = pol_re * flow + pol_im * swapped(flow)
    turned_shade = swapped(shade)
    sums = [
        jnp.sum(product, axis=0, keepdims=True)
        for product in (shade * own, turned_shade * own, shade * resid, turned_shade * resid)
    ]
    eight = lax.broadcasted_iota(jnp.int32, (8, 128), 0)
    stacked = jnp.zeros((8, 128), jnp.float32)
    for i, row in enumerate(sums):
        stacked = jnp.where(eight == i, row, stacked)
    stacked = fold(stacked)
    eight_group = lanes(8) // 16
    own_row = jnp.sum(jnp.where(eight_group == eight, stacked, 0.0), axis=0, keepdims=True)


    pl.semaphore_wait(barrier, Z + D - 2)
    @pl.when(z < HALF)
    def _():
        lax.fori_loop(1, LAST + 1, functools.partial(send_spot, 2), 0, unroll=True)
        lax.fori_loop(LAST + 1, HALF + 1, functools.partial(send_spot, 9), 0, unroll=True)
        lax.fori_loop(1, HALF + 1, functools.partial(send_src, 3), 0, unroll=True)
        lax.fori_loop(1, D, send_here, 0, unroll=True)
        lax.fori_loop(HALF + 1, Z, functools.partial(send_spot, 1), 0, unroll=True)

    @pl.when(z >= HALF)
    def _():
        lax.fori_loop(1, D, send_here, 0, unroll=True)
        lax.fori_loop(HALF + 1, Z, functools.partial(send_spot, 1), 0, unroll=True)
        lax.fori_loop(1, LAST + 1, functools.partial(send_spot, 2), 0, unroll=True)
        lax.fori_loop(LAST + 1, HALF + 1, functools.partial(send_spot, 9), 0, unroll=True)
        lax.fori_loop(1, HALF + 1, functools.partial(send_src, 3), 0, unroll=True)

    lax.fori_loop(HALF + 1, Z, functools.partial(send_src, 4), 0, unroll=True)
    lax.fori_loop(1, D, send_tgt, 0, unroll=True)

    drain(0, here_all, D - 1)
    for part in range(T // 128):
        eight_rows = here_all[part * 8 : part * 8 + 8].reshape(8, 128)
        for i in range(3):
            tiled = fold(jnp.where(eight_group == i, eight_rows, 0.0))
            picked = jnp.sum(jnp.where(eight_group == eight, tiled, 0.0), axis=0, keepdims=True)
            axes_t[i : i + 1, part * 128 : part * 128 + 128] = picked

    def spread_spots(j, carry):
        row = spot_all[j]
        for i in range(3):
            col = jnp.sum(jnp.where((group == i) & diagonal, row, 0.0), axis=1, keepdims=True)
            axes_s[i, pl.ds(pl.multiple_of(j * SH, SH), SH), :] = jnp.broadcast_to(col, (SH, 128))
        return carry

    def fill(j, carry):
        place = pl.ds(pl.multiple_of(j * SH, SH), SH)
        wide_t = T // 2
        sx, sy, sz = (jnp.tile(axes_s[i, place, :], (1, wide_t // 128)) for i in range(3))
        for part in range(2):
            cols = slice(part * wide_t, (part + 1) * wide_t)
            tx, ty, tz = (axes_t[i : i + 1, cols] for i in range(3))
            for which, value in enumerate(green(tx, ty, tz, sx, sy, sz)):
                high = value.astype(jnp.bfloat16)
                ghi[which, place, cols] = high
                glo[which, place, cols] = (value - high.astype(jnp.float32)).astype(jnp.bfloat16)
        return carry

    def two(array, comp):
        return [rows(array, 0, comp), rows(array, 1, comp)]

    def products(part):
        span = slice(part * (S // 2), (part + 1) * (S // 2))
        flows = src_all[part * HALF : (part + 1) * HALF].reshape(S // 2, 128).T
        f_hi = flows.astype(jnp.bfloat16)
        f_lo = (flows - f_hi.astype(jnp.float32)).astype(jnp.bfloat16)
        sums = [[0.0, 0.0, 0.0], [0.0, 0.0, 0.0]]
        for which, (a, b) in enumerate(PAIRS):
            high = two(f_hi, a) if a == b else two(f_hi, b) + two(f_hi, a)
            low = two(f_lo, a) if a == b else two(f_lo, b) + two(f_lo, a)
            height = 16 * len(high)
            both = jnp.concatenate(high + low, axis=0)
            high = both[:height]
            for ri in range(2):
                one = jnp.dot(both, ghi[2 * which + ri, span, :], preferred_element_type=jnp.float32)
                other = jnp.dot(high, glo[2 * which + ri, span, :], preferred_element_type=jnp.float32)
                got = one[:height] + one[height:] + other
                sums[ri][a] = sums[ri][a] + got[:32]
                if a != b:
                    sums[ri][b] = sums[ri][b] + got[32:]
        field_re = [sums[0][i][:16] - sums[1][i][16:] for i in range(3)]
        field_im = [sums[0][i][16:] + sums[1][i][:16] for i in range(3)]
        return field_re + field_im

    drain(1, spot_all, Z - 1 - HALF)
    lax.fori_loop(0, HALF, spread_spots, 0, unroll=True)
    lax.fori_loop(0, HALF, fill, 0)
    drain(9, spot_all, HALF - LAST)
    for first, end in ((HALF, FIRST_LAST), (FIRST_LAST + LAST, Z)):
        lax.fori_loop(first, end, spread_spots, 0, unroll=True)
        lax.fori_loop(first, end, fill, 0)
    drain(4, src_all, Z - 1 - HALF)
    fields[0:PLANES, :] = jnp.concatenate(products(0), axis=0)
    fields[PLANES:128, :] = jnp.zeros((128 - PLANES, T), jnp.float32)
    drain(2, spot_all, LAST)
    lax.fori_loop(FIRST_LAST, FIRST_LAST + LAST, spread_spots, 0, unroll=True)
    lax.fori_loop(FIRST_LAST, FIRST_LAST + LAST, fill, 0)
    drain(5, tgt_all, D - 1)
    tgt_t[...] = tgt_all[...].reshape(T, 128).T
    drain(3, src_all, HALF)
    parts = products(1)
    den_re = den_im = 0.0
    for i in range(3):
        sr, si = rows(tgt_t, 0, i), rows(tgt_t, 1, i)
        re, im = rows(fields, 0, i) + parts[i], rows(fields, 1, i) + parts[3 + i]
        den_re = den_re + sr * re + si * im
        den_im = den_im + sr * im - si * re
        fields[i * 16 : i * 16 + 16, :] = re
        fields[48 + i * 16 : 64 + i * 16, :] = im
    den_re = jnp.sum(den_re, axis=1, keepdims=True)
    den_im = jnp.sum(den_im, axis=1, keepdims=True)
    spread = jnp.where(group == 0, den_re, jnp.where(group == 1, den_im, 0.0))
    den_all[q] = own_row - jnp.sum(jnp.where(diagonal, spread, 0.0), axis=0, keepdims=True)

    def send_den(i, carry):
        copy(6, den_all.at[q], den_all.at[q], {"row": z * 2 + 1, "col": wrap(c + i, C)}).start()
        return carry

    def send_field(i, carry):
        other, device_id = plane_peer(i)
        copy(7, rs_send.at[other], rs_recv.at[q], device_id).start()
        return carry

    def send_fin(i, carry):
        slot = far_peer(i)[0]
        peer = lead_peer(i, 1)
        copy(8, fin_all.at[OWN], fin_all.at[slot], lead_peer(i, 0)).start()

        @pl.when(jnp.logical_not((c == 0) & (peer["row"] == 1)))
        def _():
            copy(8, fin_all.at[OWN], fin_all.at[slot], peer).start()

        return carry

    def of(which, buffer, count):
        whole = buffer.at[pl.ds(0, count)]
        return copy(which, whole, whole, far_peer(1)[1])

    COUNT = 2 * Z * C
    first = (r == 1) & (c == 0)
    others = jnp.logical_not(first)
    me = r * C + c

    @pl.when(others)
    def _():
        copy(10, den_all.at[q], every.at[me], {"row": 1, "col": 0}).start()

    @pl.when(first)
    def _():
        every[me] = den_all[q]

    @pl.when(core == 0)
    def _():
        lax.fori_loop(0, C, send_den, 0)

    @pl.when(core == 1)
    def _():
        lax.fori_loop(1, C, send_den, 0)

    rs_send[...] = fields[...].T.reshape(D, SH, 128)
    lax.fori_loop(1, D, send_field, 0)
    rs_recv[q] = rs_send[q]

    @pl.when(core == 1)
    def _():
        of(6, den_all, D - 1).wait_recv()
        fin_all[OWN] = jnp.sum(den_all[...], axis=0)
        lax.fori_loop(1, Z, send_fin, 0, unroll=True)
        copy(8, fin_all.at[OWN], fin_all.at[OWN], {"row": z * 2}).start()

    drain(7, rs_recv, D - 1)
    image = own - jnp.sum(rs_recv[...], axis=0)
    turned = swapped(image)
    img_out[...] = image[:, 0:PLANES]

    @pl.when(first)
    def _():
        of(10, every, COUNT - 1).wait_recv()

        def add(i, carry):
            return carry + jnp.sum(every[pl.ds(i * SH, SH)], axis=0)

        total[...] = lax.fori_loop(0, COUNT // SH, add, jnp.zeros((1, 128), jnp.float32), unroll=4)

    @pl.when(others)
    def _():
        of(10, every, 1).wait_send()

    @pl.when(core == 0)
    def _():
        of(6, den_all, C).wait_send()
        of(8, fin_all, Z).wait_recv()
        total[...] = jnp.sum(fin_all[...], axis=0)

    @pl.when(core == 1)
    def _():
        of(6, den_all, C - 1).wait_send()

    skips = (core == 1) & (c == 0) & (z != 0)

    @pl.when((core == 1) & jnp.logical_not(skips))
    def _():
        of(8, den_all, 2 * Z - 1).wait_send()

    @pl.when(skips)
    def _():
        of(8, den_all, 2 * Z - 2).wait_send()

    @pl.when((core == 1) & others)
    def _():
        of(8, fin_all, Z - 1).wait_recv()
        total[...] = jnp.sum(fin_all[...], axis=0)

    ends = total[...]
    ends = fold(jnp.where(eight_group == eight, ends, 0.0))
    den_re, den_im, rho_re, rho_im = (ends[i : i + 1] for i in range(4))
    magnitude = jnp.maximum(den_re * den_re + den_im * den_im, 1.0)
    alpha_re = (rho_re * den_re + rho_im * den_im) / magnitude
    alpha_im = (rho_im * den_re - rho_re * den_im) / magnitude
    half_out[...] = (resid - (alpha_re * image + alpha_im * turned))[:, 0:PLANES]


def deliver(image, half, image_out, half_out, sems):
    copies = [pltpu.make_async_copy(image, image_out, sems.at[0]), pltpu.make_async_copy(half, half_out, sems.at[1])]
    for one in copies:
        one.start()
    for one in copies:
        one.wait()


def local(R, C, currents, residual, shadow, lattice_sites, classes, inverse_polarizability):
    f32 = jnp.float32
    Z, D = R // 2, 2 * C
    T, S = D * SH, Z * SH
    shape = jax.ShapeDtypeStruct((SH, PLANES), f32)
    blocks = pl.pallas_call(
        functools.partial(body, Z, C),
        out_shape=(pltpu.VMEM((SH, PLANES), f32), pltpu.VMEM((SH, PLANES), f32)),
        in_specs=[pl.BlockSpec(memory_space=pltpu.HBM)] * 6,
        out_specs=(pl.BlockSpec(memory_space=pltpu.VMEM), pl.BlockSpec(memory_space=pltpu.VMEM)),
        scratch_shapes=[
            pltpu.VMEM((SH, PLANES), f32),
            pltpu.VMEM((SH, PLANES), f32),
            pltpu.VMEM((SH, PLANES), f32),
            pltpu.VMEM((3, SH), jnp.int32),
            pltpu.VMEM((1, SH), jnp.int32),
            pltpu.VMEM(inverse_polarizability.shape, f32),
            pltpu.VMEM((3, SH, 128), f32),
            pltpu.VMEM((Z, SH, 128), f32),
            pltpu.VMEM((Z, 1, 128), f32),
            pltpu.VMEM((D, 1, 128), f32),
            pltpu.VMEM((8, T), f32),
            pltpu.VMEM((3, S, 128), f32),
            pltpu.VMEM((D, SH, 128), f32),
            pltpu.VMEM((128, T), f32),
            pltpu.VMEM((128, T), f32),
            pltpu.VMEM((12, S, T), jnp.bfloat16),
            pltpu.VMEM((12, S, T), jnp.bfloat16),
            pltpu.VMEM((D, SH, 128), f32),
            pltpu.VMEM((D, SH, 128), f32),
            pltpu.VMEM((D, 1, 128), f32),
            pltpu.VMEM((Z, 1, 128), f32),
            pltpu.VMEM((R * C, 1, 128), f32),
            pltpu.VMEM((1, 128), f32),
            pltpu.SemaphoreType.DMA((6,)),
            pltpu.SemaphoreType.DMA((11,)),
            pltpu.SemaphoreType.DMA((11,)),
        ],
        compiler_params=pltpu.CompilerParams(
            collective_id=0, has_side_effects=True, vmem_limit_bytes=62 * 1024 * 1024
        ),
    )(currents.T, residual.T, shadow.T, lattice_sites, classes.reshape(1, SH), inverse_polarizability)
    image, half = pl.pallas_call(
        deliver,
        out_shape=(shape, shape),
        in_specs=[pl.BlockSpec(memory_space=pltpu.VMEM)] * 2,
        out_specs=(pl.BlockSpec(memory_space=pltpu.HBM), pl.BlockSpec(memory_space=pltpu.HBM)),
        scratch_shapes=[pltpu.SemaphoreType.DMA((2,))],
    )(*(pltpu.with_memory_space_constraint(block, pltpu.VMEM) for block in blocks))
    return image.T, half.T


def solution(mesh):
    both = ("row", "col")
    in_specs = (P(None, both), P(None, both), P(None, both), P(None, both), P(both), P())
    out_specs = (P(None, both), P(None, both))
    step = functools.partial(local, mesh.shape["row"], mesh.shape["col"])
    return jax.shard_map(step, mesh=mesh, in_specs=in_specs, out_specs=out_specs, check_vma=False)
```

```python
import functools
import math

import jax
import jax.numpy as jnp
import numpy as np
from jax import lax
from jax.experimental import pallas as pl
from jax.experimental.pallas import tpu as pltpu
from jax.sharding import PartitionSpec as P

MESH = pl.DeviceIdType.MESH
K = 0.9
SH = 16
PLANES = 96
PAIRS = ((0, 0), (1, 1), (2, 2), (0, 1), (0, 2), (1, 2))


def _fit(terms, odd):
    nodes = 0.5 * np.cos((np.arange(400) + 0.5) * np.pi / 400)
    powers = np.arange(terms) * 2 + (1 if odd else 0)
    values = np.sin(2 * np.pi * nodes) if odd else np.cos(2 * np.pi * nodes)
    solved = np.linalg.lstsq(nodes[:, None] ** powers[None, :], values, rcond=None)[0]
    return [float(x) for x in solved]


SIN = _fit(6, True)
COS = _fit(7, False)


def _horner(coefs, x):
    out = jnp.float32(coefs[-1])
    for coef in coefs[-2::-1]:
        out = out * x + jnp.float32(coef)
    return out


def green(tx, ty, tz, sx, sy, sz):
    dx, dy, dz = tx - sx, ty - sy, tz - sz
    xx, yy, zz = dx * dx, dy * dy, dz * dz
    dist_sq = xx + yy + zz
    safe = jnp.maximum(dist_sq, 1.0)
    inv = lax.rsqrt(safe)
    dist = safe * inv
    reach = inv * jnp.minimum(dist_sq, 1.0)
    turns = dist * jnp.float32(K / (2 * math.pi))
    frac = turns - jnp.round(turns)
    frac_sq = frac * frac
    e_re = _horner(COS, frac_sq) * reach
    e_im = _horner(SIN, frac_sq) * frac * reach
    inv_sq = inv * inv
    iso_re = jnp.float32(K * K) - inv_sq
    iso_im = jnp.float32(K) * inv
    a_re = e_re * iso_re - e_im * iso_im
    a_im = e_im * iso_re + e_re * iso_im
    b_re = (jnp.float32(2 * K * K) * e_re - 3.0 * a_re) * inv_sq
    b_im = (jnp.float32(2 * K * K) * e_im - 3.0 * a_im) * inv_sq
    outer = (xx, yy, zz, dx * dy, dx * dz, dy * dz)
    parts = []
    for place, product in enumerate(outer):
        re, im = product * b_re, product * b_im
        if place < 3:
            re, im = re + a_re, im + a_im
        parts.extend((re, im))
    return parts


def rows(array, b, component):
    start = b * 48 + component * 16
    return array[start : start + 16]


def lanes(height):
    return lax.broadcasted_iota(jnp.int32, (height, 128), 1)


def sublanes(height):
    return lax.broadcasted_iota(jnp.int32, (height, 128), 0)


def swapped(block):
    lane = lanes(block.shape[0])
    turned = jnp.where(lane < 48, -pltpu.roll(block, 80, 1), pltpu.roll(block, 48, 1))
    return jnp.where(lane < PLANES, turned, 0.0)


def fold(block):
    for shift in (64, 32, 16):
        block = block + pltpu.roll(block, shift, 1)
    return block


def pairwise(stack):
    while stack.shape[0] > 1:
        half = stack.shape[0] // 2
        stack = stack[:half] + stack[half:]
    return stack[0]


def body(
    Z, C,
    cur_hbm, res_hbm, sha_hbm, site_hbm, cls_hbm, pol_hbm,
    img_out, half_out,
    cur, res, sha, site, cls, pol,
    wide, src_all, spot_all, here_all, axes_t, axes_s, tgt_all, tgt_t, fields, ghi, glo, rs_send, rs_recv, den_all, fin_all, every, total,
    in_sems, send_sems, recv_sems,
):
    r, c = lax.axis_index("row"), lax.axis_index("col")
    z, core = r // 2, r % 2
    D = 2 * C
    q = core * C + c
    T, S = D * SH, Z * SH

    def wrap(i, size):
        return jnp.where(i >= size, i - size, i)

    def plane_peer(i):
        other = wrap(q + i, D)
        upper = other >= C
        return other, {"row": z * 2 + jnp.where(upper, 1, 0), "col": jnp.where(upper, other - C, other)}

    HALF, OWN = Z // 2, Z // 4
    LAST = 3 if Z > 4 else 1
    FIRST_LAST = OWN + HALF - LAST // 2

    def far_peer(i):
        step = jnp.where(i % 2 == 0, HALF + i // 2, HALF - i // 2)
        return wrap(OWN - step + Z, Z), {"row": wrap(z + step, Z) * 2 + core}

    def lead_peer(i, to_core):
        step = jnp.where(i % 2 == 0, HALF + i // 2, HALF - i // 2)
        return {"row": wrap(z + step, Z) * 2 + to_core}

    barrier = pltpu.get_barrier_semaphore()

    def greet_far(i, carry):
        pl.semaphore_signal(barrier, inc=1, device_id=far_peer(i)[1], device_id_type=MESH)
        return carry

    def greet_plane(i, carry):
        pl.semaphore_signal(barrier, inc=1, device_id=plane_peer(i)[1], device_id_type=MESH)
        return carry

    lax.fori_loop(1, Z, greet_far, 0)

    lax.fori_loop(1, D, greet_plane, 0)

    pairs = ((cur_hbm, cur), (res_hbm, res), (sha_hbm, sha), (site_hbm, site), (cls_hbm, cls), (pol_hbm, pol))
    loads = [pltpu.make_async_copy(a, b, in_sems.at[i]) for i, (a, b) in enumerate(pairs)]
    for load in loads:
        load.start()

    wide[...] = jnp.zeros_like(wide)
    for load in loads:
        load.wait()

    for i, ref in enumerate((cur, res, sha)):
        wide[i, :, 0:PLANES] = ref[...]
    lane, sublane = lanes(SH), sublanes(SH)
    group, diagonal = lane // 16, lane % 16 == sublane
    small_lane = lax.broadcasted_iota(jnp.int32, (SH, SH), 1)
    small_sublane = lax.broadcasted_iota(jnp.int32, (SH, SH), 0)

    def column(row):
        return jnp.sum(jnp.where(small_lane == small_sublane, row, 0.0), axis=1, keepdims=True)

    flow, resid, shade = wide[0], wide[1], wide[2]
    spots = site[...].astype(jnp.float32)
    axes = [column(spots[i : i + 1]) for i in range(3)]
    block = shade
    spot_row = jnp.zeros((SH, 128), jnp.float32)
    for i in range(3):
        block = jnp.where(lane == PLANES + i, axes[i], block)
        spot_row = jnp.where((group == i) & diagonal, axes[i], spot_row)
    tgt_all[q] = block
    spot_row = jnp.sum(spot_row, axis=0, keepdims=True)
    spot_all[OWN] = spot_row
    here_all[q] = spot_row
    src_all[OWN] = flow

    def copy(which, src, dst, device_id):
        return pltpu.make_async_remote_copy(
            src_ref=src, dst_ref=dst, send_sem=send_sems.at[which], recv_sem=recv_sems.at[which],
            device_id=device_id, device_id_type=MESH,
        )

    def send_here(i, carry):
        copy(0, here_all.at[q], here_all.at[q], plane_peer(i)[1]).start()
        return carry

    def send_spot(which, i, carry):
        slot, device_id = far_peer(i)
        copy(which, spot_all.at[OWN], spot_all.at[slot], device_id).start()
        return carry

    def send_src(which, i, carry):
        slot, device_id = far_peer(i)
        copy(which, src_all.at[OWN], src_all.at[slot], device_id).start()
        return carry

    def send_tgt(i, carry):
        copy(5, tgt_all.at[q], tgt_all.at[q], plane_peer(i)[1]).start()
        return carry

    def drain(which, buffer, count):
        whole = buffer.at[pl.ds(0, count)]
        copy(which, whole, whole, far_peer(1)[1]).wait()

    class_col = column(cls[...].astype(jnp.float32))
    pol_re = jnp.zeros((SH, 1), jnp.float32)
    pol_im = jnp.zeros((SH, 1), jnp.float32)
    for kind in range(pol.shape[1]):
        pol_re = jnp.where(class_col == kind, pol[0:1, kind : kind + 1], pol_re)
        pol_im = jnp.where(class_col == kind, pol[1:2, kind : kind + 1], pol_im)
    own = pol_re * flow + pol_im * swapped(flow)
    turned_shade = swapped(shade)
    sums = [
        jnp.sum(product, axis=0, keepdims=True)
        for product in (shade * own, turned_shade * own, shade * resid, turned_shade * resid)
    ]
    eight = lax.broadcasted_iota(jnp.int32, (8, 128), 0)
    stacked = jnp.zeros((8, 128), jnp.float32)
    for i, row in enumerate(sums):
        stacked = jnp.where(eight == i, row, stacked)
    stacked = fold(stacked)
    eight_group = lanes(8) // 16
    own_row = jnp.sum(jnp.where(eight_group == eight, stacked, 0.0), axis=0, keepdims=True)


    pl.semaphore_wait(barrier, Z + D - 2)
    @pl.when(z < HALF)
    def _():
        lax.fori_loop(1, LAST + 1, functools.partial(send_spot, 2), 0, unroll=True)
        lax.fori_loop(LAST + 1, HALF + 1, functools.partial(send_spot, 9), 0, unroll=True)
        lax.fori_loop(1, HALF + 1, functools.partial(send_src, 3), 0, unroll=True)
        lax.fori_loop(1, D, send_here, 0, unroll=True)
        lax.fori_loop(HALF + 1, Z, functools.partial(send_spot, 1), 0, unroll=True)

    @pl.when(z >= HALF)
    def _():
        lax.fori_loop(1, D, send_here, 0, unroll=True)
        lax.fori_loop(HALF + 1, Z, functools.partial(send_spot, 1), 0, unroll=True)
        lax.fori_loop(1, LAST + 1, functools.partial(send_spot, 2), 0, unroll=True)
        lax.fori_loop(LAST + 1, HALF + 1, functools.partial(send_spot, 9), 0, unroll=True)
        lax.fori_loop(1, HALF + 1, functools.partial(send_src, 3), 0, unroll=True)

    lax.fori_loop(HALF + 1, Z, functools.partial(send_src, 4), 0, unroll=True)
    lax.fori_loop(1, D, send_tgt, 0, unroll=True)

    drain(0, here_all, D - 1)
    for part in range(T // 128):
        eight_rows = here_all[part * 8 : part * 8 + 8].reshape(8, 128)
        for i in range(3):
            tiled = fold(jnp.where(eight_group == i, eight_rows, 0.0))
            picked = jnp.sum(jnp.where(eight_group == eight, tiled, 0.0), axis=0, keepdims=True)
            axes_t[i : i + 1, part * 128 : part * 128 + 128] = picked

    def spread_spots(j, carry):
        row = spot_all[j]
        for i in range(3):
            col = jnp.sum(jnp.where((group == i) & diagonal, row, 0.0), axis=1, keepdims=True)
            axes_s[i, pl.ds(pl.multiple_of(j * SH, SH), SH), :] = jnp.broadcast_to(col, (SH, 128))
        return carry

    def fill(j, carry):
        place = pl.ds(pl.multiple_of(j * SH, SH), SH)
        wide_t = T // 2
        sx, sy, sz = (jnp.tile(axes_s[i, place, :], (1, wide_t // 128)) for i in range(3))
        for part in range(2):
            cols = slice(part * wide_t, (part + 1) * wide_t)
            tx, ty, tz = (axes_t[i : i + 1, cols] for i in range(3))
            for which, value in enumerate(green(tx, ty, tz, sx, sy, sz)):
                high = value.astype(jnp.bfloat16)
                ghi[which, place, cols] = high
                glo[which, place, cols] = (value - high.astype(jnp.float32)).astype(jnp.bfloat16)
        return carry

    def two(array, comp):
        return [rows(array, 0, comp), rows(array, 1, comp)]

    def products(part):
        span = slice(part * (S // 2), (part + 1) * (S // 2))
        flows = src_all[part * HALF : (part + 1) * HALF].reshape(S // 2, 128).T
        f_hi = flows.astype(jnp.bfloat16)
        f_lo = (flows - f_hi.astype(jnp.float32)).astype(jnp.bfloat16)
        sums = [[0.0, 0.0, 0.0], [0.0, 0.0, 0.0]]
        for which, (a, b) in enumerate(PAIRS):
            high = two(f_hi, a) if a == b else two(f_hi, b) + two(f_hi, a)
            low = two(f_lo, a) if a == b else two(f_lo, b) + two(f_lo, a)
            height = 16 * len(high)
            both = jnp.concatenate(high + low, axis=0)
            high = both[:height]
            for ri in range(2):
                one = jnp.dot(both, ghi[2 * which + ri, span, :], preferred_element_type=jnp.float32)
                other = jnp.dot(high, glo[2 * which + ri, span, :], preferred_element_type=jnp.float32)
                got = one[:height] + one[height:] + other
                sums[ri][a] = sums[ri][a] + got[:32]
                if a != b:
                    sums[ri][b] = sums[ri][b] + got[32:]
        field_re = [sums[0][i][:16] - sums[1][i][16:] for i in range(3)]
        field_im = [sums[0][i][16:] + sums[1][i][:16] for i in range(3)]
        return field_re + field_im

    drain(1, spot_all, Z - 1 - HALF)
    lax.fori_loop(0, HALF, spread_spots, 0, unroll=True)
    lax.fori_loop(0, HALF, fill, 0)
    drain(9, spot_all, HALF - LAST)
    for first, end in ((HALF, FIRST_LAST), (FIRST_LAST + LAST, Z)):
        lax.fori_loop(first, end, spread_spots, 0, unroll=True)
        lax.fori_loop(first, end, fill, 0)
    drain(4, src_all, Z - 1 - HALF)
    fields[0:PLANES, :] = jnp.concatenate(products(0), axis=0)
    fields[PLANES:128, :] = jnp.zeros((128 - PLANES, T), jnp.float32)
    drain(2, spot_all, LAST)
    lax.fori_loop(FIRST_LAST, FIRST_LAST + LAST, spread_spots, 0, unroll=True)
    lax.fori_loop(FIRST_LAST, FIRST_LAST + LAST, fill, 0)
    drain(5, tgt_all, D - 1)
    tgt_t[...] = tgt_all[...].reshape(T, 128).T
    drain(3, src_all, HALF)
    parts = products(1)
    den_re = den_im = 0.0
    for i in range(3):
        sr, si = rows(tgt_t, 0, i), rows(tgt_t, 1, i)
        re, im = rows(fields, 0, i) + parts[i], rows(fields, 1, i) + parts[3 + i]
        den_re = den_re + sr * re + si * im
        den_im = den_im + sr * im - si * re
        fields[i * 16 : i * 16 + 16, :] = re
        fields[48 + i * 16 : 64 + i * 16, :] = im
    den_re = jnp.sum(den_re, axis=1, keepdims=True)
    den_im = jnp.sum(den_im, axis=1, keepdims=True)
    spread = jnp.where(group == 0, den_re, jnp.where(group == 1, den_im, 0.0))
    den_all[q] = own_row - jnp.sum(jnp.where(diagonal, spread, 0.0), axis=0, keepdims=True)

    def send_den(i, carry):
        copy(6, den_all.at[q], den_all.at[q], {"row": z * 2 + 1, "col": wrap(c + i, C)}).start()
        return carry

    def send_field(i, carry):
        other, device_id = plane_peer(i)
        copy(7, rs_send.at[other], rs_recv.at[q], device_id).start()
        return carry

    def send_fin(i, carry):
        slot = far_peer(i)[0]
        peer = lead_peer(i, 1)
        copy(8, fin_all.at[OWN], fin_all.at[slot], lead_peer(i, 0)).start()

        @pl.when(jnp.logical_not((c == 0) & (peer["row"] == 1)))
        def _():
            copy(8, fin_all.at[OWN], fin_all.at[slot], peer).start()

        return carry

    def of(which, buffer, count):
        whole = buffer.at[pl.ds(0, count)]
        return copy(which, whole, whole, far_peer(1)[1])

    COUNT = 2 * Z * C
    first = (r == 1) & (c == 0)
    others = jnp.logical_not(first)
    me = r * C + c

    @pl.when(others)
    def _():
        copy(10, den_all.at[q], every.at[me], {"row": 1, "col": 0}).start()

    @pl.when(first)
    def _():
        every[me] = den_all[q]

    @pl.when(core == 0)
    def _():
        lax.fori_loop(0, C, send_den, 0)

    @pl.when(core == 1)
    def _():
        lax.fori_loop(1, C, send_den, 0)

    rs_send[...] = fields[...].T.reshape(D, SH, 128)
    lax.fori_loop(1, D, send_field, 0)
    rs_recv[q] = rs_send[q]

    @pl.when(core == 1)
    def _():
        of(6, den_all, D - 1).wait_recv()
        fin_all[OWN] = pairwise(den_all[...])
        lax.fori_loop(1, Z, send_fin, 0, unroll=True)
        copy(8, fin_all.at[OWN], fin_all.at[OWN], {"row": z * 2}).start()

    drain(7, rs_recv, D - 1)
    image = own - jnp.sum(rs_recv[...], axis=0)
    turned = swapped(image)
    img_out[...] = image[:, 0:PLANES]

    @pl.when(first)
    def _():
        of(10, every, COUNT - 1).wait_recv()

        def add(i, carry):
            return carry + every[pl.ds(i * SH, SH)]

        sixteen = lax.fori_loop(1, COUNT // SH, add, every[0:SH], unroll=True)
        total[...] = pairwise(sixteen)

    @pl.when(others)
    def _():
        of(10, every, 1).wait_send()

    @pl.when(core == 0)
    def _():
        of(6, den_all, C).wait_send()
        of(8, fin_all, Z).wait_recv()
        total[...] = pairwise(fin_all[...])

    @pl.when(core == 1)
    def _():
        of(6, den_all, C - 1).wait_send()

    skips = (core == 1) & (c == 0) & (z != 0)

    @pl.when((core == 1) & jnp.logical_not(skips))
    def _():
        of(8, den_all, 2 * Z - 1).wait_send()

    @pl.when(skips)
    def _():
        of(8, den_all, 2 * Z - 2).wait_send()

    @pl.when((core == 1) & others)
    def _():
        of(8, fin_all, Z - 1).wait_recv()
        total[...] = pairwise(fin_all[...])

    ends = total[...]
    ends = fold(jnp.where(eight_group == eight, ends, 0.0))
    den_re, den_im, rho_re, rho_im = (ends[i : i + 1] for i in range(4))
    magnitude = jnp.maximum(den_re * den_re + den_im * den_im, 1.0)
    alpha_re = (rho_re * den_re + rho_im * den_im) / magnitude
    alpha_im = (rho_im * den_re - rho_re * den_im) / magnitude
    half_out[...] = (resid - (alpha_re * image + alpha_im * turned))[:, 0:PLANES]


def deliver(image, half, image_out, half_out, sems):
    copies = [pltpu.make_async_copy(image, image_out, sems.at[0]), pltpu.make_async_copy(half, half_out, sems.at[1])]
    for one in copies:
        one.start()
    for one in copies:
        one.wait()


def local(R, C, currents, residual, shadow, lattice_sites, classes, inverse_polarizability):
    f32 = jnp.float32
    Z, D = R // 2, 2 * C
    T, S = D * SH, Z * SH
    shape = jax.ShapeDtypeStruct((SH, PLANES), f32)
    blocks = pl.pallas_call(
        functools.partial(body, Z, C),
        out_shape=(pltpu.VMEM((SH, PLANES), f32), pltpu.VMEM((SH, PLANES), f32)),
        in_specs=[pl.BlockSpec(memory_space=pltpu.HBM)] * 6,
        out_specs=(pl.BlockSpec(memory_space=pltpu.VMEM), pl.BlockSpec(memory_space=pltpu.VMEM)),
        scratch_shapes=[
            pltpu.VMEM((SH, PLANES), f32),
            pltpu.VMEM((SH, PLANES), f32),
            pltpu.VMEM((SH, PLANES), f32),
            pltpu.VMEM((3, SH), jnp.int32),
            pltpu.VMEM((1, SH), jnp.int32),
            pltpu.VMEM(inverse_polarizability.shape, f32),
            pltpu.VMEM((3, SH, 128), f32),
            pltpu.VMEM((Z, SH, 128), f32),
            pltpu.VMEM((Z, 1, 128), f32),
            pltpu.VMEM((D, 1, 128), f32),
            pltpu.VMEM((8, T), f32),
            pltpu.VMEM((3, S, 128), f32),
            pltpu.VMEM((D, SH, 128), f32),
            pltpu.VMEM((128, T), f32),
            pltpu.VMEM((128, T), f32),
            pltpu.VMEM((12, S, T), jnp.bfloat16),
            pltpu.VMEM((12, S, T), jnp.bfloat16),
            pltpu.VMEM((D, SH, 128), f32),
            pltpu.VMEM((D, SH, 128), f32),
            pltpu.VMEM((D, 1, 128), f32),
            pltpu.VMEM((Z, 1, 128), f32),
            pltpu.VMEM((R * C, 1, 128), f32),
            pltpu.VMEM((1, 128), f32),
            pltpu.SemaphoreType.DMA((6,)),
            pltpu.SemaphoreType.DMA((11,)),
            pltpu.SemaphoreType.DMA((11,)),
        ],
        compiler_params=pltpu.CompilerParams(
            collective_id=0, has_side_effects=True, vmem_limit_bytes=62 * 1024 * 1024
        ),
    )(currents.T, residual.T, shadow.T, lattice_sites, classes.reshape(1, SH), inverse_polarizability)
    image, half = pl.pallas_call(
        deliver,
        out_shape=(shape, shape),
        in_specs=[pl.BlockSpec(memory_space=pltpu.VMEM)] * 2,
        out_specs=(pl.BlockSpec(memory_space=pltpu.HBM), pl.BlockSpec(memory_space=pltpu.HBM)),
        scratch_shapes=[pltpu.SemaphoreType.DMA((2,))],
    )(*(pltpu.with_memory_space_constraint(block, pltpu.VMEM) for block in blocks))
    return image.T, half.T


def solution(mesh):
    both = ("row", "col")
    in_specs = (P(None, both), P(None, both), P(None, both), P(None, both), P(both), P())
    out_specs = (P(None, both), P(None, both))
    step = functools.partial(local, mesh.shape["row"], mesh.shape["col"])
    return jax.shard_map(step, mesh=mesh, in_specs=in_specs, out_specs=out_specs, check_vma=False)
```

```python
import functools
import math

import jax
import jax.numpy as jnp
import numpy as np
from jax import lax
from jax.experimental import pallas as pl
from jax.experimental.pallas import tpu as pltpu
from jax.sharding import PartitionSpec as P

MESH = pl.DeviceIdType.MESH
K = 0.9
SH = 16
PLANES = 96
PAIRS = ((0, 0), (1, 1), (2, 2), (0, 1), (0, 2), (1, 2))


def _fit(terms, odd):
    nodes = 0.5 * np.cos((np.arange(400) + 0.5) * np.pi / 400)
    powers = np.arange(terms) * 2 + (1 if odd else 0)
    values = np.sin(2 * np.pi * nodes) if odd else np.cos(2 * np.pi * nodes)
    solved = np.linalg.lstsq(nodes[:, None] ** powers[None, :], values, rcond=None)[0]
    return [float(x) for x in solved]


SIN = _fit(6, True)
COS = _fit(7, False)


def _horner(coefs, x):
    out = jnp.float32(coefs[-1])
    for coef in coefs[-2::-1]:
        out = out * x + jnp.float32(coef)
    return out


def green(tx, ty, tz, sx, sy, sz):
    dx, dy, dz = tx - sx, ty - sy, tz - sz
    xx, yy, zz = dx * dx, dy * dy, dz * dz
    dist_sq = xx + yy + zz
    safe = jnp.maximum(dist_sq, 1.0)
    inv = lax.rsqrt(safe)
    dist = safe * inv
    reach = inv * jnp.minimum(dist_sq, 1.0)
    turns = dist * jnp.float32(K / (2 * math.pi))
    frac = turns - jnp.round(turns)
    frac_sq = frac * frac
    e_re = _horner(COS, frac_sq) * reach
    e_im = _horner(SIN, frac_sq) * frac * reach
    inv_sq = inv * inv
    iso_re = jnp.float32(K * K) - inv_sq
    iso_im = jnp.float32(K) * inv
    a_re = e_re * iso_re - e_im * iso_im
    a_im = e_im * iso_re + e_re * iso_im
    b_re = (jnp.float32(2 * K * K) * e_re - 3.0 * a_re) * inv_sq
    b_im = (jnp.float32(2 * K * K) * e_im - 3.0 * a_im) * inv_sq
    outer = (xx, yy, zz, dx * dy, dx * dz, dy * dz)
    parts = []
    for place, product in enumerate(outer):
        re, im = product * b_re, product * b_im
        if place < 3:
            re, im = re + a_re, im + a_im
        parts.extend((re, im))
    return parts


def rows(array, b, component):
    start = b * 48 + component * 16
    return array[start : start + 16]


def lanes(height):
    return lax.broadcasted_iota(jnp.int32, (height, 128), 1)


def sublanes(height):
    return lax.broadcasted_iota(jnp.int32, (height, 128), 0)


def swapped(block):
    lane = lanes(block.shape[0])
    turned = jnp.where(lane < 48, -pltpu.roll(block, 80, 1), pltpu.roll(block, 48, 1))
    return jnp.where(lane < PLANES, turned, 0.0)


def fold(block):
    for shift in (64, 32, 16):
        block = block + pltpu.roll(block, shift, 1)
    return block


def pairwise(stack):
    while stack.shape[0] > 1:
        half = stack.shape[0] // 2
        stack = stack[:half] + stack[half:]
    return stack[0]


def body(
    Z, C,
    cur_hbm, res_hbm, sha_hbm, site_hbm, cls_hbm, pol_hbm,
    img_out, half_out,
    cur, res, sha, site, cls, pol,
    wide, src_all, spot_all, here_all, axes_t, axes_s, tgt_all, tgt_t, fields, ghi, glo, rs_send, rs_recv, den_all, fin_all, every, total, den_near,
    in_sems, send_sems, recv_sems,
):
    r, c = lax.axis_index("row"), lax.axis_index("col")
    z, core = r // 2, r % 2
    D = 2 * C
    q = core * C + c
    T, S = D * SH, Z * SH

    def wrap(i, size):
        return jnp.where(i >= size, i - size, i)

    def plane_peer(i):
        other = wrap(q + i, D)
        upper = other >= C
        return other, {"row": z * 2 + jnp.where(upper, 1, 0), "col": jnp.where(upper, other - C, other)}

    HALF, OWN = Z // 2, Z // 4
    LAST = 3 if Z > 4 else 1
    FIRST_LAST = OWN + HALF - LAST // 2

    def far_peer(i):
        step = jnp.where(i % 2 == 0, HALF + i // 2, HALF - i // 2)
        return wrap(OWN - step + Z, Z), {"row": wrap(z + step, Z) * 2 + core}

    def lead_peer(i, to_core):
        step = jnp.where(i % 2 == 0, HALF + i // 2, HALF - i // 2)
        return {"row": wrap(z + step, Z) * 2 + to_core}

    barrier = pltpu.get_barrier_semaphore()

    def greet_far(i, carry):
        pl.semaphore_signal(barrier, inc=1, device_id=far_peer(i)[1], device_id_type=MESH)
        return carry

    def greet_plane(i, carry):
        pl.semaphore_signal(barrier, inc=1, device_id=plane_peer(i)[1], device_id_type=MESH)
        return carry

    lax.fori_loop(1, Z, greet_far, 0)

    lax.fori_loop(1, D, greet_plane, 0)

    pairs = ((cur_hbm, cur), (res_hbm, res), (sha_hbm, sha), (site_hbm, site), (cls_hbm, cls), (pol_hbm, pol))
    loads = [pltpu.make_async_copy(a, b, in_sems.at[i]) for i, (a, b) in enumerate(pairs)]
    for load in loads:
        load.start()

    wide[...] = jnp.zeros_like(wide)
    for load in loads:
        load.wait()

    for i, ref in enumerate((cur, res, sha)):
        wide[i, :, 0:PLANES] = ref[...]
    lane, sublane = lanes(SH), sublanes(SH)
    group, diagonal = lane // 16, lane % 16 == sublane
    small_lane = lax.broadcasted_iota(jnp.int32, (SH, SH), 1)
    small_sublane = lax.broadcasted_iota(jnp.int32, (SH, SH), 0)

    def column(row):
        return jnp.sum(jnp.where(small_lane == small_sublane, row, 0.0), axis=1, keepdims=True)

    flow, resid, shade = wide[0], wide[1], wide[2]
    spots = site[...].astype(jnp.float32)
    axes = [column(spots[i : i + 1]) for i in range(3)]
    block = shade
    spot_row = jnp.zeros((SH, 128), jnp.float32)
    for i in range(3):
        block = jnp.where(lane == PLANES + i, axes[i], block)
        spot_row = jnp.where((group == i) & diagonal, axes[i], spot_row)
    tgt_all[q] = block
    spot_row = jnp.sum(spot_row, axis=0, keepdims=True)
    spot_all[OWN] = spot_row
    here_all[q] = spot_row
    src_all[OWN] = flow

    def copy(which, src, dst, device_id):
        return pltpu.make_async_remote_copy(
            src_ref=src, dst_ref=dst, send_sem=send_sems.at[which], recv_sem=recv_sems.at[which],
            device_id=device_id, device_id_type=MESH,
        )

    def send_here(i, carry):
        copy(0, here_all.at[q], here_all.at[q], plane_peer(i)[1]).start()
        return carry

    def send_spot(which, i, carry):
        slot, device_id = far_peer(i)
        copy(which, spot_all.at[OWN], spot_all.at[slot], device_id).start()
        return carry

    def send_src(which, i, carry):
        slot, device_id = far_peer(i)
        copy(which, src_all.at[OWN], src_all.at[slot], device_id).start()
        return carry

    def send_tgt(i, carry):
        copy(5, tgt_all.at[q], tgt_all.at[q], plane_peer(i)[1]).start()
        return carry

    def drain(which, buffer, count):
        whole = buffer.at[pl.ds(0, count)]
        copy(which, whole, whole, far_peer(1)[1]).wait()

    class_col = column(cls[...].astype(jnp.float32))
    pol_re = jnp.zeros((SH, 1), jnp.float32)
    pol_im = jnp.zeros((SH, 1), jnp.float32)
    for kind in range(pol.shape[1]):
        pol_re = jnp.where(class_col == kind, pol[0:1, kind : kind + 1], pol_re)
        pol_im = jnp.where(class_col == kind, pol[1:2, kind : kind + 1], pol_im)
    own = pol_re * flow + pol_im * swapped(flow)
    turned_shade = swapped(shade)
    sums = [
        jnp.sum(product, axis=0, keepdims=True)
        for product in (shade * own, turned_shade * own, shade * resid, turned_shade * resid)
    ]
    eight = lax.broadcasted_iota(jnp.int32, (8, 128), 0)
    stacked = jnp.zeros((8, 128), jnp.float32)
    for i, row in enumerate(sums):
        stacked = jnp.where(eight == i, row, stacked)
    stacked = fold(stacked)
    eight_group = lanes(8) // 16
    own_row = jnp.sum(jnp.where(eight_group == eight, stacked, 0.0), axis=0, keepdims=True)


    pl.semaphore_wait(barrier, Z + D - 2)
    @pl.when(z < HALF)
    def _():
        lax.fori_loop(1, LAST + 1, functools.partial(send_spot, 2), 0, unroll=True)
        lax.fori_loop(LAST + 1, HALF + 1, functools.partial(send_spot, 9), 0, unroll=True)
        lax.fori_loop(1, HALF + 1, functools.partial(send_src, 3), 0, unroll=True)
        lax.fori_loop(1, D, send_here, 0, unroll=True)
        lax.fori_loop(HALF + 1, Z, functools.partial(send_spot, 1), 0, unroll=True)

    @pl.when(z >= HALF)
    def _():
        lax.fori_loop(1, D, send_here, 0, unroll=True)
        lax.fori_loop(HALF + 1, Z, functools.partial(send_spot, 1), 0, unroll=True)
        lax.fori_loop(1, LAST + 1, functools.partial(send_spot, 2), 0, unroll=True)
        lax.fori_loop(LAST + 1, HALF + 1, functools.partial(send_spot, 9), 0, unroll=True)
        lax.fori_loop(1, HALF + 1, functools.partial(send_src, 3), 0, unroll=True)

    lax.fori_loop(HALF + 1, Z, functools.partial(send_src, 4), 0, unroll=True)
    lax.fori_loop(1, D, send_tgt, 0, unroll=True)

    drain(0, here_all, D - 1)
    for part in range(T // 128):
        eight_rows = here_all[part * 8 : part * 8 + 8].reshape(8, 128)
        for i in range(3):
            tiled = fold(jnp.where(eight_group == i, eight_rows, 0.0))
            picked = jnp.sum(jnp.where(eight_group == eight, tiled, 0.0), axis=0, keepdims=True)
            axes_t[i : i + 1, part * 128 : part * 128 + 128] = picked

    def spread_spots(j, carry):
        row = spot_all[j]
        for i in range(3):
            col = jnp.sum(jnp.where((group == i) & diagonal, row, 0.0), axis=1, keepdims=True)
            axes_s[i, pl.ds(pl.multiple_of(j * SH, SH), SH), :] = jnp.broadcast_to(col, (SH, 128))
        return carry

    def fill(j, carry):
        place = pl.ds(pl.multiple_of(j * SH, SH), SH)
        wide_t = T // 2
        sx, sy, sz = (jnp.tile(axes_s[i, place, :], (1, wide_t // 128)) for i in range(3))
        for part in range(2):
            cols = slice(part * wide_t, (part + 1) * wide_t)
            tx, ty, tz = (axes_t[i : i + 1, cols] for i in range(3))
            for which, value in enumerate(green(tx, ty, tz, sx, sy, sz)):
                high = value.astype(jnp.bfloat16)
                ghi[which, place, cols] = high
                glo[which, place, cols] = (value - high.astype(jnp.float32)).astype(jnp.bfloat16)
        return carry

    def two(array, comp):
        return [rows(array, 0, comp), rows(array, 1, comp)]

    def products(part):
        span = slice(part * (S // 2), (part + 1) * (S // 2))
        flows = src_all[part * HALF : (part + 1) * HALF].reshape(S // 2, 128).T
        f_hi = flows.astype(jnp.bfloat16)
        f_lo = (flows - f_hi.astype(jnp.float32)).astype(jnp.bfloat16)
        sums = [[0.0, 0.0, 0.0], [0.0, 0.0, 0.0]]
        for which, (a, b) in enumerate(PAIRS):
            high = two(f_hi, a) if a == b else two(f_hi, b) + two(f_hi, a)
            low = two(f_lo, a) if a == b else two(f_lo, b) + two(f_lo, a)
            height = 16 * len(high)
            both = jnp.concatenate(high + low, axis=0)
            high = both[:height]
            for ri in range(2):
                one = jnp.dot(both, ghi[2 * which + ri, span, :], preferred_element_type=jnp.float32)
                other = jnp.dot(high, glo[2 * which + ri, span, :], preferred_element_type=jnp.float32)
                got = one[:height] + one[height:] + other
                sums[ri][a] = sums[ri][a] + got[:32]
                if a != b:
                    sums[ri][b] = sums[ri][b] + got[32:]
        field_re = [sums[0][i][:16] - sums[1][i][16:] for i in range(3)]
        field_im = [sums[0][i][16:] + sums[1][i][:16] for i in range(3)]
        return field_re + field_im

    drain(1, spot_all, Z - 1 - HALF)
    lax.fori_loop(0, HALF, spread_spots, 0, unroll=True)
    lax.fori_loop(0, HALF, fill, 0)
    drain(9, spot_all, HALF - LAST)
    for first, end in ((HALF, FIRST_LAST), (FIRST_LAST + LAST, Z)):
        lax.fori_loop(first, end, spread_spots, 0, unroll=True)
        lax.fori_loop(first, end, fill, 0)
    drain(4, src_all, Z - 1 - HALF)
    fields[0:PLANES, :] = jnp.concatenate(products(0), axis=0)
    fields[PLANES:128, :] = jnp.zeros((128 - PLANES, T), jnp.float32)
    drain(2, spot_all, LAST)
    lax.fori_loop(FIRST_LAST, FIRST_LAST + LAST, spread_spots, 0, unroll=True)
    lax.fori_loop(FIRST_LAST, FIRST_LAST + LAST, fill, 0)
    drain(5, tgt_all, D - 1)
    tgt_t[...] = tgt_all[...].reshape(T, 128).T
    den_re = den_im = 0.0
    for i in range(3):
        sr, si = rows(tgt_t, 0, i), rows(tgt_t, 1, i)
        re, im = rows(fields, 0, i), rows(fields, 1, i)
        den_re = den_re + sr * re + si * im
        den_im = den_im + sr * im - si * re
    den_near[0], den_near[1] = den_re, den_im
    drain(3, src_all, HALF)
    den_re, den_im = den_near[0], den_near[1]
    parts = products(1)
    for i in range(3):
        sr, si = rows(tgt_t, 0, i), rows(tgt_t, 1, i)
        den_re = den_re + sr * parts[i] + si * parts[3 + i]
        den_im = den_im + sr * parts[3 + i] - si * parts[i]
    den_re = jnp.sum(den_re, axis=1, keepdims=True)
    den_im = jnp.sum(den_im, axis=1, keepdims=True)
    spread = jnp.where(group == 0, den_re, jnp.where(group == 1, den_im, 0.0))
    den_all[q] = own_row - jnp.sum(jnp.where(diagonal, spread, 0.0), axis=0, keepdims=True)

    def send_den(i, carry):
        copy(6, den_all.at[q], den_all.at[q], {"row": z * 2 + 1, "col": wrap(c + i, C)}).start()
        return carry

    def send_field(i, carry):
        other, device_id = plane_peer(i)
        copy(7, rs_send.at[other], rs_recv.at[q], device_id).start()
        return carry

    def send_fin(i, carry):
        slot = far_peer(i)[0]
        peer = lead_peer(i, 1)
        copy(8, fin_all.at[OWN], fin_all.at[slot], lead_peer(i, 0)).start()

        @pl.when(jnp.logical_not((c == 0) & (peer["row"] == 1)))
        def _():
            copy(8, fin_all.at[OWN], fin_all.at[slot], peer).start()

        return carry

    def of(which, buffer, count):
        whole = buffer.at[pl.ds(0, count)]
        return copy(which, whole, whole, far_peer(1)[1])

    COUNT = 2 * Z * C
    first = (r == 1) & (c == 0)
    others = jnp.logical_not(first)
    me = r * C + c

    @pl.when(others)
    def _():
        copy(10, den_all.at[q], every.at[me], {"row": 1, "col": 0}).start()

    @pl.when(first)
    def _():
        every[me] = den_all[q]

    @pl.when(core == 0)
    def _():
        lax.fori_loop(0, C, send_den, 0, unroll=True)

    @pl.when(core == 1)
    def _():
        lax.fori_loop(1, C, send_den, 0, unroll=True)

    fields[0:PLANES, :] += jnp.concatenate(parts, axis=0)
    rs_send[...] = fields[...].T.reshape(D, SH, 128)
    lax.fori_loop(1, D, send_field, 0)
    rs_recv[q] = rs_send[q]

    @pl.when(core == 1)
    def _():
        of(6, den_all, D - 1).wait_recv()
        fin_all[OWN] = pairwise(den_all[...])
        lax.fori_loop(1, Z, send_fin, 0, unroll=True)
        copy(8, fin_all.at[OWN], fin_all.at[OWN], {"row": z * 2}).start()

    drain(7, rs_recv, D - 1)
    image = own - jnp.sum(rs_recv[...], axis=0)
    turned = swapped(image)
    img_out[...] = image[:, 0:PLANES]

    @pl.when(first)
    def _():
        of(10, every, COUNT - 1).wait_recv()

        def add(i, carry):
            return carry + every[pl.ds(i * SH, SH)]

        sixteen = lax.fori_loop(1, COUNT // SH, add, every[0:SH], unroll=True)
        total[...] = pairwise(sixteen)

    @pl.when(others)
    def _():
        of(10, every, 1).wait_send()

    @pl.when(core == 0)
    def _():
        of(6, den_all, C).wait_send()
        of(8, fin_all, Z).wait_recv()
        total[...] = pairwise(fin_all[...])

    @pl.when(core == 1)
    def _():
        of(6, den_all, C - 1).wait_send()

    skips = (core == 1) & (c == 0) & (z != 0)

    @pl.when((core == 1) & jnp.logical_not(skips))
    def _():
        of(8, den_all, 2 * Z - 1).wait_send()

    @pl.when(skips)
    def _():
        of(8, den_all, 2 * Z - 2).wait_send()

    @pl.when((core == 1) & others)
    def _():
        of(8, fin_all, Z - 1).wait_recv()
        total[...] = pairwise(fin_all[...])

    ends = total[...]
    ends = fold(jnp.where(eight_group == eight, ends, 0.0))
    den_re, den_im, rho_re, rho_im = (ends[i : i + 1] for i in range(4))
    magnitude = jnp.maximum(den_re * den_re + den_im * den_im, 1.0)
    alpha_re = (rho_re * den_re + rho_im * den_im) / magnitude
    alpha_im = (rho_im * den_re - rho_re * den_im) / magnitude
    half_out[...] = (resid - (alpha_re * image + alpha_im * turned))[:, 0:PLANES]


def deliver(image, half, image_out, half_out, sems):
    copies = [pltpu.make_async_copy(image, image_out, sems.at[0]), pltpu.make_async_copy(half, half_out, sems.at[1])]
    for one in copies:
        one.start()
    for one in copies:
        one.wait()


def local(R, C, currents, residual, shadow, lattice_sites, classes, inverse_polarizability):
    f32 = jnp.float32
    Z, D = R // 2, 2 * C
    T, S = D * SH, Z * SH
    shape = jax.ShapeDtypeStruct((SH, PLANES), f32)
    blocks = pl.pallas_call(
        functools.partial(body, Z, C),
        out_shape=(pltpu.VMEM((SH, PLANES), f32), pltpu.VMEM((SH, PLANES), f32)),
        in_specs=[pl.BlockSpec(memory_space=pltpu.HBM)] * 6,
        out_specs=(pl.BlockSpec(memory_space=pltpu.VMEM), pl.BlockSpec(memory_space=pltpu.VMEM)),
        scratch_shapes=[
            pltpu.VMEM((SH, PLANES), f32),
            pltpu.VMEM((SH, PLANES), f32),
            pltpu.VMEM((SH, PLANES), f32),
            pltpu.VMEM((3, SH), jnp.int32),
            pltpu.VMEM((1, SH), jnp.int32),
            pltpu.VMEM(inverse_polarizability.shape, f32),
            pltpu.VMEM((3, SH, 128), f32),
            pltpu.VMEM((Z, SH, 128), f32),
            pltpu.VMEM((Z, 1, 128), f32),
            pltpu.VMEM((D, 1, 128), f32),
            pltpu.VMEM((8, T), f32),
            pltpu.VMEM((3, S, 128), f32),
            pltpu.VMEM((D, SH, 128), f32),
            pltpu.VMEM((128, T), f32),
            pltpu.VMEM((128, T), f32),
            pltpu.VMEM((12, S, T), jnp.bfloat16),
            pltpu.VMEM((12, S, T), jnp.bfloat16),
            pltpu.VMEM((D, SH, 128), f32),
            pltpu.VMEM((D, SH, 128), f32),
            pltpu.VMEM((D, 1, 128), f32),
            pltpu.VMEM((Z, 1, 128), f32),
            pltpu.VMEM((R * C, 1, 128), f32),
            pltpu.VMEM((1, 128), f32),
            pltpu.VMEM((2, SH, T), f32),
            pltpu.SemaphoreType.DMA((6,)),
            pltpu.SemaphoreType.DMA((11,)),
            pltpu.SemaphoreType.DMA((11,)),
        ],
        compiler_params=pltpu.CompilerParams(
            collective_id=0, has_side_effects=True, vmem_limit_bytes=62 * 1024 * 1024
        ),
    )(currents.T, residual.T, shadow.T, lattice_sites, classes.reshape(1, SH), inverse_polarizability)
    image, half = pl.pallas_call(
        deliver,
        out_shape=(shape, shape),
        in_specs=[pl.BlockSpec(memory_space=pltpu.VMEM)] * 2,
        out_specs=(pl.BlockSpec(memory_space=pltpu.HBM), pl.BlockSpec(memory_space=pltpu.HBM)),
        scratch_shapes=[pltpu.SemaphoreType.DMA((2,))],
    )(*(pltpu.with_memory_space_constraint(block, pltpu.VMEM) for block in blocks))
    return image.T, half.T


def solution(mesh):
    both = ("row", "col")
    in_specs = (P(None, both), P(None, both), P(None, both), P(None, both), P(both), P())
    out_specs = (P(None, both), P(None, both))
    step = functools.partial(local, mesh.shape["row"], mesh.shape["col"])
    return jax.shard_map(step, mesh=mesh, in_specs=in_specs, out_specs=out_specs, check_vma=False)
```

```python
import functools
import math

import jax
import jax.numpy as jnp
import numpy as np
from jax import lax
from jax.experimental import pallas as pl
from jax.experimental.pallas import tpu as pltpu
from jax.sharding import PartitionSpec as P

MESH = pl.DeviceIdType.MESH
K = 0.9
SH = 16
PLANES = 96
PAIRS = ((0, 0), (1, 1), (2, 2), (0, 1), (0, 2), (1, 2))


def _fit(terms, odd):
    nodes = 0.5 * np.cos((np.arange(400) + 0.5) * np.pi / 400)
    powers = np.arange(terms) * 2 + (1 if odd else 0)
    values = np.sin(2 * np.pi * nodes) if odd else np.cos(2 * np.pi * nodes)
    solved = np.linalg.lstsq(nodes[:, None] ** powers[None, :], values, rcond=None)[0]
    return [float(x) for x in solved]


SIN = _fit(6, True)
COS = _fit(7, False)


def _horner(coefs, x):
    out = jnp.float32(coefs[-1])
    for coef in coefs[-2::-1]:
        out = out * x + jnp.float32(coef)
    return out


def green(tx, ty, tz, sx, sy, sz):
    dx, dy, dz = tx - sx, ty - sy, tz - sz
    xx, yy, zz = dx * dx, dy * dy, dz * dz
    dist_sq = xx + yy + zz
    safe = jnp.maximum(dist_sq, 1.0)
    inv = lax.rsqrt(safe)
    dist = safe * inv
    reach = inv * jnp.minimum(dist_sq, 1.0)
    turns = dist * jnp.float32(K / (2 * math.pi))
    frac = turns - jnp.round(turns)
    frac_sq = frac * frac
    e_re = _horner(COS, frac_sq) * reach
    e_im = _horner(SIN, frac_sq) * frac * reach
    inv_sq = inv * inv
    iso_re = jnp.float32(K * K) - inv_sq
    iso_im = jnp.float32(K) * inv
    a_re = e_re * iso_re - e_im * iso_im
    a_im = e_im * iso_re + e_re * iso_im
    b_re = (jnp.float32(2 * K * K) * e_re - 3.0 * a_re) * inv_sq
    b_im = (jnp.float32(2 * K * K) * e_im - 3.0 * a_im) * inv_sq
    outer = (xx, yy, zz, dx * dy, dx * dz, dy * dz)
    parts = []
    for place, product in enumerate(outer):
        re, im = product * b_re, product * b_im
        if place < 3:
            re, im = re + a_re, im + a_im
        parts.extend((re, im))
    return parts


def rows(array, b, component):
    start = b * 48 + component * 16
    return array[start : start + 16]


def lanes(height):
    return lax.broadcasted_iota(jnp.int32, (height, 128), 1)


def sublanes(height):
    return lax.broadcasted_iota(jnp.int32, (height, 128), 0)


def swapped(block):
    lane = lanes(block.shape[0])
    turned = jnp.where(lane < 48, -pltpu.roll(block, 80, 1), pltpu.roll(block, 48, 1))
    return jnp.where(lane < PLANES, turned, 0.0)


def fold(block):
    for shift in (64, 32, 16):
        block = block + pltpu.roll(block, shift, 1)
    return block


def pairwise(stack):
    while stack.shape[0] > 1:
        half = stack.shape[0] // 2
        stack = stack[:half] + stack[half:]
    return stack[0]


def body(
    Z, C,
    cur_hbm, res_hbm, sha_hbm, site_hbm, cls_hbm, pol_hbm,
    img_out, half_out,
    cur, res, sha, site, cls, pol,
    wide, src_all, spot_all, here_all, axes_t, axes_s, tgt_all, tgt_t, fields, ghi, glo, rs_send, rs_recv, den_all, fin_all, every, total,
    in_sems, send_sems, recv_sems,
):
    r, c = lax.axis_index("row"), lax.axis_index("col")
    z, core = r // 2, r % 2
    D = 2 * C
    q = core * C + c
    T, S = D * SH, Z * SH

    def wrap(i, size):
        return jnp.where(i >= size, i - size, i)

    def plane_peer(i):
        other = wrap(q + i, D)
        upper = other >= C
        return other, {"row": z * 2 + jnp.where(upper, 1, 0), "col": jnp.where(upper, other - C, other)}

    HALF, OWN = Z // 2, Z // 4
    LAST = 3 if Z > 4 else 1
    FIRST_LAST = OWN + HALF - LAST // 2

    def far_peer(i):
        step = jnp.where(i % 2 == 0, HALF + i // 2, HALF - i // 2)
        return wrap(OWN - step + Z, Z), {"row": wrap(z + step, Z) * 2 + core}

    def lead_peer(i, to_core):
        step = jnp.where(i % 2 == 0, HALF + i // 2, HALF - i // 2)
        return {"row": wrap(z + step, Z) * 2 + to_core}

    barrier = pltpu.get_barrier_semaphore()

    def greet_far(i, carry):
        pl.semaphore_signal(barrier, inc=1, device_id=far_peer(i)[1], device_id_type=MESH)
        return carry

    def greet_plane(i, carry):
        pl.semaphore_signal(barrier, inc=1, device_id=plane_peer(i)[1], device_id_type=MESH)
        return carry

    lax.fori_loop(1, Z, greet_far, 0)

    lax.fori_loop(1, D, greet_plane, 0)

    pairs = ((cur_hbm, cur), (res_hbm, res), (sha_hbm, sha), (site_hbm, site), (cls_hbm, cls), (pol_hbm, pol))
    loads = [pltpu.make_async_copy(a, b, in_sems.at[i]) for i, (a, b) in enumerate(pairs)]
    for load in loads:
        load.start()

    wide[...] = jnp.zeros_like(wide)
    for load in loads:
        load.wait()

    for i, ref in enumerate((cur, res, sha)):
        wide[i, :, 0:PLANES] = ref[...]
    lane, sublane = lanes(SH), sublanes(SH)
    group, diagonal = lane // 16, lane % 16 == sublane
    small_lane = lax.broadcasted_iota(jnp.int32, (SH, SH), 1)
    small_sublane = lax.broadcasted_iota(jnp.int32, (SH, SH), 0)

    def column(row):
        return jnp.sum(jnp.where(small_lane == small_sublane, row, 0.0), axis=1, keepdims=True)

    flow, resid, shade = wide[0], wide[1], wide[2]
    spots = site[...].astype(jnp.float32)
    axes = [column(spots[i : i + 1]) for i in range(3)]
    block = shade
    spot_row = jnp.zeros((SH, 128), jnp.float32)
    for i in range(3):
        block = jnp.where(lane == PLANES + i, axes[i], block)
        spot_row = jnp.where((group == i) & diagonal, axes[i], spot_row)
    tgt_all[q] = block
    spot_row = jnp.sum(spot_row, axis=0, keepdims=True)
    spot_all[OWN] = spot_row
    here_all[q] = spot_row
    src_all[OWN] = flow

    def copy(which, src, dst, device_id):
        return pltpu.make_async_remote_copy(
            src_ref=src, dst_ref=dst, send_sem=send_sems.at[which], recv_sem=recv_sems.at[which],
            device_id=device_id, device_id_type=MESH,
        )

    def send_here(i, carry):
        copy(0, here_all.at[q], here_all.at[q], plane_peer(i)[1]).start()
        return carry

    def send_spot(which, i, carry):
        slot, device_id = far_peer(i)
        copy(which, spot_all.at[OWN], spot_all.at[slot], device_id).start()
        return carry

    def send_src(which, i, carry):
        slot, device_id = far_peer(i)
        copy(which, src_all.at[OWN], src_all.at[slot], device_id).start()
        return carry

    def send_tgt(i, carry):
        copy(5, tgt_all.at[q], tgt_all.at[q], plane_peer(i)[1]).start()
        return carry

    def drain(which, buffer, count):
        whole = buffer.at[pl.ds(0, count)]
        copy(which, whole, whole, far_peer(1)[1]).wait()

    class_col = column(cls[...].astype(jnp.float32))
    pol_re = jnp.zeros((SH, 1), jnp.float32)
    pol_im = jnp.zeros((SH, 1), jnp.float32)
    for kind in range(pol.shape[1]):
        pol_re = jnp.where(class_col == kind, pol[0:1, kind : kind + 1], pol_re)
        pol_im = jnp.where(class_col == kind, pol[1:2, kind : kind + 1], pol_im)
    own = pol_re * flow + pol_im * swapped(flow)
    turned_shade = swapped(shade)
    sums = [
        jnp.sum(product, axis=0, keepdims=True)
        for product in (shade * own, turned_shade * own, shade * resid, turned_shade * resid)
    ]
    eight = lax.broadcasted_iota(jnp.int32, (8, 128), 0)
    stacked = jnp.zeros((8, 128), jnp.float32)
    for i, row in enumerate(sums):
        stacked = jnp.where(eight == i, row, stacked)
    stacked = fold(stacked)
    eight_group = lanes(8) // 16
    own_row = jnp.sum(jnp.where(eight_group == eight, stacked, 0.0), axis=0, keepdims=True)


    pl.semaphore_wait(barrier, Z + D - 2)
    @pl.when(z < HALF)
    def _():
        lax.fori_loop(1, LAST + 1, functools.partial(send_spot, 2), 0, unroll=True)
        lax.fori_loop(LAST + 1, HALF + 1, functools.partial(send_spot, 9), 0, unroll=True)
        lax.fori_loop(1, HALF + 1, functools.partial(send_src, 3), 0, unroll=True)
        lax.fori_loop(1, D, send_here, 0, unroll=True)
        lax.fori_loop(HALF + 1, Z, functools.partial(send_spot, 1), 0, unroll=True)

    @pl.when(z >= HALF)
    def _():
        lax.fori_loop(1, D, send_here, 0, unroll=True)
        lax.fori_loop(HALF + 1, Z, functools.partial(send_spot, 1), 0, unroll=True)
        lax.fori_loop(1, LAST + 1, functools.partial(send_spot, 2), 0, unroll=True)
        lax.fori_loop(LAST + 1, HALF + 1, functools.partial(send_spot, 9), 0, unroll=True)
        lax.fori_loop(1, HALF + 1, functools.partial(send_src, 3), 0, unroll=True)

    lax.fori_loop(HALF + 1, Z, functools.partial(send_src, 4), 0, unroll=True)
    lax.fori_loop(1, D, send_tgt, 0, unroll=True)

    drain(0, here_all, D - 1)
    for part in range(T // 128):
        eight_rows = here_all[part * 8 : part * 8 + 8].reshape(8, 128)
        for i in range(3):
            tiled = fold(jnp.where(eight_group == i, eight_rows, 0.0))
            picked = jnp.sum(jnp.where(eight_group == eight, tiled, 0.0), axis=0, keepdims=True)
            axes_t[i : i + 1, part * 128 : part * 128 + 128] = picked

    def spread_spots(j, carry):
        row = spot_all[j]
        for i in range(3):
            col = jnp.sum(jnp.where((group == i) & diagonal, row, 0.0), axis=1, keepdims=True)
            axes_s[i, pl.ds(pl.multiple_of(j * SH, SH), SH), :] = jnp.broadcast_to(col, (SH, 128))
        return carry

    def fill(j, carry):
        place = pl.ds(pl.multiple_of(j * SH, SH), SH)
        wide_t = T // 2
        sx, sy, sz = (jnp.tile(axes_s[i, place, :], (1, wide_t // 128)) for i in range(3))
        for part in range(2):
            cols = slice(part * wide_t, (part + 1) * wide_t)
            tx, ty, tz = (axes_t[i : i + 1, cols] for i in range(3))
            for which, value in enumerate(green(tx, ty, tz, sx, sy, sz)):
                high = value.astype(jnp.bfloat16)
                ghi[which, place, cols] = high
                glo[which, place, cols] = (value - high.astype(jnp.float32)).astype(jnp.bfloat16)
        return carry

    def two(array, comp):
        return [rows(array, 0, comp), rows(array, 1, comp)]

    def products(part):
        span = slice(part * (S // 2), (part + 1) * (S // 2))
        flows = src_all[part * HALF : (part + 1) * HALF].reshape(S // 2, 128).T
        f_hi = flows.astype(jnp.bfloat16)
        f_lo = (flows - f_hi.astype(jnp.float32)).astype(jnp.bfloat16)
        sums = [[0.0, 0.0, 0.0], [0.0, 0.0, 0.0]]
        for which, (a, b) in enumerate(PAIRS):
            high = two(f_hi, a) if a == b else two(f_hi, b) + two(f_hi, a)
            low = two(f_lo, a) if a == b else two(f_lo, b) + two(f_lo, a)
            height = 16 * len(high)
            both = jnp.concatenate(high + low, axis=0)
            high = both[:height]
            for ri in range(2):
                one = jnp.dot(both, ghi[2 * which + ri, span, :], preferred_element_type=jnp.float32)
                other = jnp.dot(high, glo[2 * which + ri, span, :], preferred_element_type=jnp.float32)
                got = one[:height] + one[height:] + other
                sums[ri][a] = sums[ri][a] + got[:32]
                if a != b:
                    sums[ri][b] = sums[ri][b] + got[32:]
        field_re = [sums[0][i][:16] - sums[1][i][16:] for i in range(3)]
        field_im = [sums[0][i][16:] + sums[1][i][:16] for i in range(3)]
        return field_re + field_im

    drain(1, spot_all, Z - 1 - HALF)
    lax.fori_loop(0, HALF, spread_spots, 0, unroll=True)
    lax.fori_loop(0, HALF, fill, 0)
    drain(9, spot_all, HALF - LAST)
    for first, end in ((HALF, FIRST_LAST), (FIRST_LAST + LAST, Z)):
        lax.fori_loop(first, end, spread_spots, 0, unroll=True)
        lax.fori_loop(first, end, fill, 0)
    drain(4, src_all, Z - 1 - HALF)
    fields[0:PLANES, :] = jnp.concatenate(products(0), axis=0)
    fields[PLANES:128, :] = jnp.zeros((128 - PLANES, T), jnp.float32)
    drain(2, spot_all, LAST)
    lax.fori_loop(FIRST_LAST, FIRST_LAST + LAST, spread_spots, 0, unroll=True)
    lax.fori_loop(FIRST_LAST, FIRST_LAST + LAST, fill, 0)
    drain(5, tgt_all, D - 1)
    tgt_t[...] = tgt_all[...].reshape(T, 128).T
    drain(3, src_all, HALF)
    parts = products(1)
    den_re = den_im = 0.0
    for i in range(3):
        sr, si = rows(tgt_t, 0, i), rows(tgt_t, 1, i)
        re, im = rows(fields, 0, i) + parts[i], rows(fields, 1, i) + parts[3 + i]
        den_re = den_re + sr * re + si * im
        den_im = den_im + sr * im - si * re
        fields[i * 16 : i * 16 + 16, :] = re
        fields[48 + i * 16 : 64 + i * 16, :] = im
    den_re = jnp.sum(den_re, axis=1, keepdims=True)
    den_im = jnp.sum(den_im, axis=1, keepdims=True)
    spread = jnp.where(group == 0, den_re, jnp.where(group == 1, den_im, 0.0))
    den_all[q] = own_row - jnp.sum(jnp.where(diagonal, spread, 0.0), axis=0, keepdims=True)

    def send_den(i, carry):
        copy(6, den_all.at[q], den_all.at[q], {"row": z * 2 + 1, "col": wrap(c + i, C)}).start()
        return carry

    def send_field(i, carry):
        other, device_id = plane_peer(i)
        copy(7, rs_send.at[other], rs_recv.at[q], device_id).start()
        return carry

    def send_fin(i, carry):
        slot = far_peer(i)[0]
        peer = lead_peer(i, 1)
        copy(8, fin_all.at[OWN], fin_all.at[slot], lead_peer(i, 0)).start()

        @pl.when(jnp.logical_not((c == 0) & (peer["row"] == 1)))
        def _():
            copy(8, fin_all.at[OWN], fin_all.at[slot], peer).start()

        return carry

    def of(which, buffer, count):
        whole = buffer.at[pl.ds(0, count)]
        return copy(which, whole, whole, far_peer(1)[1])

    COUNT = 2 * Z * C
    first = (r == 1) & (c == 0)
    others = jnp.logical_not(first)
    me = r * C + c

    @pl.when(others)
    def _():
        copy(10, den_all.at[q], every.at[me], {"row": 1, "col": 0}).start()

    @pl.when(first)
    def _():
        every[me] = den_all[q]

    @pl.when(core == 0)
    def _():
        lax.fori_loop(0, C, send_den, 0, unroll=True)

    @pl.when(core == 1)
    def _():
        lax.fori_loop(1, C, send_den, 0, unroll=True)

    rs_send[...] = fields[...].T.reshape(D, SH, 128)
    lax.fori_loop(1, D, send_field, 0)
    rs_recv[q] = rs_send[q]

    @pl.when(core == 1)
    def _():
        of(6, den_all, D - 1).wait_recv()
        fin_all[OWN] = pairwise(den_all[...])
        lax.fori_loop(1, Z, send_fin, 0, unroll=True)
        copy(8, fin_all.at[OWN], fin_all.at[OWN], {"row": z * 2}).start()

    drain(7, rs_recv, D - 1)
    image = own - jnp.sum(rs_recv[...], axis=0)
    turned = swapped(image)
    img_out[...] = image[:, 0:PLANES]

    @pl.when(first)
    def _():
        of(10, every, COUNT - 1).wait_recv()

        def add(i, carry):
            return carry + every[pl.ds(i * SH, SH)]

        sixteen = lax.fori_loop(1, COUNT // SH, add, every[0:SH], unroll=True)
        total[...] = pairwise(sixteen)

    @pl.when(others)
    def _():
        of(10, every, 1).wait_send()

    @pl.when(core == 0)
    def _():
        of(6, den_all, C).wait_send()
        of(8, fin_all, Z).wait_recv()
        total[...] = pairwise(fin_all[...])

    @pl.when(core == 1)
    def _():
        of(6, den_all, C - 1).wait_send()

    skips = (core == 1) & (c == 0) & (z != 0)

    @pl.when((core == 1) & jnp.logical_not(skips))
    def _():
        of(8, den_all, 2 * Z - 1).wait_send()

    @pl.when(skips)
    def _():
        of(8, den_all, 2 * Z - 2).wait_send()

    @pl.when((core == 1) & others)
    def _():
        of(8, fin_all, Z - 1).wait_recv()
        total[...] = pairwise(fin_all[...])

    ends = total[...]
    ends = fold(jnp.where(eight_group == eight, ends, 0.0))
    den_re, den_im, rho_re, rho_im = (ends[i : i + 1] for i in range(4))
    magnitude = jnp.maximum(den_re * den_re + den_im * den_im, 1.0)
    alpha_re = (rho_re * den_re + rho_im * den_im) / magnitude
    alpha_im = (rho_im * den_re - rho_re * den_im) / magnitude
    half_out[...] = (resid - (alpha_re * image + alpha_im * turned))[:, 0:PLANES]


def deliver(image, half, image_out, half_out, sems):
    copies = [pltpu.make_async_copy(image, image_out, sems.at[0]), pltpu.make_async_copy(half, half_out, sems.at[1])]
    for one in copies:
        one.start()
    for one in copies:
        one.wait()


def local(R, C, currents, residual, shadow, lattice_sites, classes, inverse_polarizability):
    f32 = jnp.float32
    Z, D = R // 2, 2 * C
    T, S = D * SH, Z * SH
    shape = jax.ShapeDtypeStruct((SH, PLANES), f32)
    blocks = pl.pallas_call(
        functools.partial(body, Z, C),
        out_shape=(pltpu.VMEM((SH, PLANES), f32), pltpu.VMEM((SH, PLANES), f32)),
        in_specs=[pl.BlockSpec(memory_space=pltpu.HBM)] * 6,
        out_specs=(pl.BlockSpec(memory_space=pltpu.VMEM), pl.BlockSpec(memory_space=pltpu.VMEM)),
        scratch_shapes=[
            pltpu.VMEM((SH, PLANES), f32),
            pltpu.VMEM((SH, PLANES), f32),
            pltpu.VMEM((SH, PLANES), f32),
            pltpu.VMEM((3, SH), jnp.int32),
            pltpu.VMEM((1, SH), jnp.int32),
            pltpu.VMEM(inverse_polarizability.shape, f32),
            pltpu.VMEM((3, SH, 128), f32),
            pltpu.VMEM((Z, SH, 128), f32),
            pltpu.VMEM((Z, 1, 128), f32),
            pltpu.VMEM((D, 1, 128), f32),
            pltpu.VMEM((8, T), f32),
            pltpu.VMEM((3, S, 128), f32),
            pltpu.VMEM((D, SH, 128), f32),
            pltpu.VMEM((128, T), f32),
            pltpu.VMEM((128, T), f32),
            pltpu.VMEM((12, S, T), jnp.bfloat16),
            pltpu.VMEM((12, S, T), jnp.bfloat16),
            pltpu.VMEM((D, SH, 128), f32),
            pltpu.VMEM((D, SH, 128), f32),
            pltpu.VMEM((D, 1, 128), f32),
            pltpu.VMEM((Z, 1, 128), f32),
            pltpu.VMEM((R * C, 1, 128), f32),
            pltpu.VMEM((1, 128), f32),
            pltpu.SemaphoreType.DMA((6,)),
            pltpu.SemaphoreType.DMA((11,)),
            pltpu.SemaphoreType.DMA((11,)),
        ],
        compiler_params=pltpu.CompilerParams(
            collective_id=0, has_side_effects=True, vmem_limit_bytes=62 * 1024 * 1024
        ),
    )(currents.T, residual.T, shadow.T, lattice_sites, classes.reshape(1, SH), inverse_polarizability)
    image, half = pl.pallas_call(
        deliver,
        out_shape=(shape, shape),
        in_specs=[pl.BlockSpec(memory_space=pltpu.VMEM)] * 2,
        out_specs=(pl.BlockSpec(memory_space=pltpu.HBM), pl.BlockSpec(memory_space=pltpu.HBM)),
        scratch_shapes=[pltpu.SemaphoreType.DMA((2,))],
    )(*(pltpu.with_memory_space_constraint(block, pltpu.VMEM) for block in blocks))
    return image.T, half.T


def solution(mesh):
    both = ("row", "col")
    in_specs = (P(None, both), P(None, both), P(None, both), P(None, both), P(both), P())
    out_specs = (P(None, both), P(None, both))
    step = functools.partial(local, mesh.shape["row"], mesh.shape["col"])
    return jax.shard_map(step, mesh=mesh, in_specs=in_specs, out_specs=out_specs, check_vma=False)
```
